32 devices in a mesh: groups: 2 (over y), replica: 4 (over z), tensor: 4 (over x, core).
Axes of the slice: x: 2, y: 2, z: 4, core: 2. Of those that a mesh axis runs over, the one named last changes fastest.
Arguments:
- activations: bfloat16 [256, 8192], P(('groups', 'replica'), 'tensor'), parts along dimension 0, may hold values from -6 to 6
- value_matrix: bfloat16 [8192, 1024], P('tensor'), may hold values from -0.0625 to 0.0625
- value_offset_bias: float32 [1024], P('tensor'), may hold values from -3 to 3
- adapter_down_factors: bfloat16 [32, 64, 8192], P(('groups', 'replica'), None, 'tensor'), parts along dimension 0, may hold values from -0.0625 to 0.0625
- adapter_up_factors: bfloat16 [32, 64, 1024], P(('groups', 'replica')), parts along dimension 0, may hold values from -0.75 to 0.75
- adapter_replica: int32 [256, 1], P(('groups', 'replica')), parts along dimension 0, may hold values from 0 to 3; in each aligned block of 32 rows (0 to 31, 32 to 63, ...) at most 16 rows name the same one
- adapter_position: int32 [256], P(('groups', 'replica')), parts along dimension 0, may hold values from 0 to 3
- queries: bfloat16 [256, 64, 128], P(('groups', 'replica'), 'tensor'), parts along dimension 0, may hold values from -88 to 88
- cached_key_rows: bfloat16 [256, 8, 96, 128], P(('groups', 'replica'), 'tensor'), parts along dimension 0, may hold values from -4 to 4
- cached_value_rows: bfloat16 [256, 8, 96, 128], P(('groups', 'replica'), 'tensor'), parts along dimension 0, may hold values from -6 to 6
- incoming_keys: bfloat16 [256, 8, 128], P(('groups', 'replica'), 'tensor'), parts along dimension 0, may hold values from -6 to 6
- lengths: int32 [256], P(('groups', 'replica')), parts along dimension 0, may hold values from 2 to 96, as said below
Outputs:
- context: bfloat16 [256, 64, 128], P(('groups', 'replica'), 'tensor'), parts along dimension 0
- incoming_values: bfloat16 [256, 8, 128], P(('groups', 'replica'), 'tensor'), parts along dimension 0
The draws below stay inside these ranges and needn't reach their ends.
There are 2 independent parts, one for each index of `groups`. The reference program is written for one: setup_inputs(seed, part) draws one part's arguments, and reference() takes and returns one part's arrays. A program takes and returns all parts, laid end to end along the dimension named above; an argument that names none is the same for every part. Nothing has to cross between parts.
Inputs may be any that keep to these rules, and one draw needn't show every extreme that they name: `adapter_replica`: among the 32 requests of one replica (aligned blocks of rows), no replica index is named by more than 16; in some blocks one is named exactly 16 times. `lengths`: some request has exactly 96 cached tokens.
All inputs are finite; a program needn't handle non-finite values.
Results may differ from the reference program's by a relative error of at most 0.0051.
Values may be sent and summed in bfloat16 or wider, within the bound.
No kernel may reach another device: no remote copies, remote signals or barrier semaphores. Data moves between devices by JAX's collectives and lax.ppermute only.
A program may use at most 64 MiB of HBM per device.

```python
import math
import jax
import jax.numpy as jnp
import numpy as np
from jax import lax

MODEL_WIDTH = 8192
QH = 64
KEY_HEADS = 8
HEAD_WIDTH = 128
ADAPTER_RANK = 64
ADP_DEV = 4
R_DEV = 32
LEN = 96
VALUE_FEATURES = 1024
REQUEST_COUNT = 128
ADAPTER_COUNT = 16
CAP = 16
N_REPLICA = 4


def key_field(key):
    field_key = jax.random.fold_in(key, 11)
    return jax.random.truncated_normal(field_key, -4.0, 4.0, (REQUEST_COUNT, KEY_HEADS, LEN, HEAD_WIDTH), jnp.float32)


def draw_cached_key_rows(key, part):
    field = key_field(key)
    return field.astype(jnp.bfloat16)


def draw_queries(key, part):
    key = jax.random.fold_in(key, 5)
    first_key = jax.random.fold_in(key, 0)
    values = jax.random.truncated_normal(first_key, -4.0, 4.0, (REQUEST_COUNT, QH, HEAD_WIDTH), jnp.float32)
    return values.astype(jnp.bfloat16)


def draw_lengths(key, part):
    key = jax.random.fold_in(key, 7)
    first_key, second_key = jax.random.split(key)
    counts = jax.random.randint(first_key, (REQUEST_COUNT,), 2, LEN + 1)
    chosen = jax.random.randint(second_key, (), 0, REQUEST_COUNT)
    counts = jnp.where(jnp.arange(REQUEST_COUNT) == chosen, LEN, counts)
    return counts.astype(jnp.int32)


def with_ends(result, stream_key, low, high):
    shape = result.shape
    spot = [jax.random.randint(jax.random.fold_in(stream_key, axis), (), 0, shape[axis]) for axis in range(len(shape))]
    result = result.at[tuple(spot)].set(low)
    longest = shape.index(max(shape))
    spot[longest] = (spot[longest] + 1) % shape[longest]
    return result.at[tuple(spot)].set(high)


def shard_levels(stream_key, extent, pieces, least, largest):
    def one(axis_at, shards_of):
        draws = jax.random.uniform(jax.random.fold_in(jax.random.fold_in(stream_key, 6), axis_at), (shards_of,), jnp.float32, least / len(pieces), largest / len(pieces))
        return jnp.repeat(jnp.exp(draws), extent[axis_at] // shards_of).reshape((-1,) + (1,) * (len(extent) - axis_at - 1))

    gain = one(*pieces[0])
    for cut in pieces[1:]:
        gain = gain * one(*cut)
    return gain


def assign_block(own_key, own, number, rows, amount, top, reach, skew):
    sequence = jax.random.permutation(own_key, amount)
    packed, usual = shares(amount, rows * top, reach, skew, True), shares(amount, rows * top, reach, skew, False)
    places = jnp.arange(amount)

    def named(sizes, rotation):
        used = int((sizes > 0).sum())
        fixed = max(1, used // 4)
        moved = fixed + (places - fixed + rotation * (used - fixed)) % max(1, amount - fixed)
        return jnp.zeros((amount,), jnp.int32).at[sequence[jnp.where(places < fixed, places, moved)]].set(jnp.asarray(sizes, jnp.int32))

    sizes = jnp.where(number % 4 == 0, named(packed, number // 4), named(usual, number - number // 4 - 1))
    mixed = jax.random.permutation(jax.random.fold_in(own, 3), amount)
    donor, taker = mixed[0:amount // 2 * 2:2], mixed[1:amount // 2 * 2:2]
    slack = jnp.minimum(sizes[donor] - 1, reach - sizes[taker]) // 2
    slack = jnp.where((donor == sequence[0]) | (taker == sequence[0]) | (sizes[taker] == 0), 0, jnp.maximum(slack, 0))
    moved = jax.random.randint(jax.random.fold_in(own, 4), (amount // 2,), 0, 1 << 20) % (slack + 1)
    sizes = sizes.at[donor].add(-moved).at[taker].add(moved)
    members = jnp.searchsorted(jnp.cumsum(sizes), jnp.arange(rows * top), side="right").astype(jnp.int32)
    listing = members.reshape(top, rows).T
    listing = listing[jax.random.permutation(jax.random.fold_in(own, 1), rows)]
    rotation = jax.random.randint(jax.random.fold_in(own, 2), (rows, 1), 0, top)
    return jnp.take_along_axis(listing, (jnp.arange(top)[None, :] + rotation) % top, axis=1)


def shares(count, total, bound, skew, full):
    portions = [(1 << 20) // math.isqrt(rank ** skew) + 1 for rank in range(1, count + 1)]
    largest = bound if full else min(bound, max(-(-total // count), total * portions[0] // sum(portions)))
    least = 1 if total - largest >= count - 1 else 0
    given, spare = [largest] + [least] * (count - 1), total - largest - least * (count - 1)
    while spare > 0:
        movable = [i for i in range(1, count) if given[i] < largest] or [i for i in range(1, count) if given[i] < bound]
        whole, budget = sum([portions[i] for i in movable]), spare
        for i in movable:
            addition = min(bound - given[i], max(1, budget * portions[i] // whole), spare)
            given[i] = given[i] + addition
            spare = spare - addition
    return np.array(given)


def gaussian(key, shape, width, limit, cuts=(), kind=jnp.bfloat16):
    drawn = jax.random.normal(key, shape, jnp.float32) * width
    if len(cuts) > 0:
        drawn = shard_levels(key, shape, cuts, -0.22, 0.18) * drawn
    return jnp.clip(drawn, min=-limit, max=limit).astype(kind)


def setup_inputs(seed: int = 0, part: int = 0) -> dict:
    key_of = jax.random.split(jax.random.key(seed), 13)
    own_keys = jax.random.split(jax.random.fold_in(key_of[12], part), 13)
    activations = gaussian(own_keys[0], (REQUEST_COUNT, MODEL_WIDTH), 1.0, 6.0, ((0, 4), (1, 4)))
    value_matrix = gaussian(key_of[1], (MODEL_WIDTH, VALUE_FEATURES), MODEL_WIDTH ** -0.5, 0.0625, ((0, 4),))
    value_offset_bias = gaussian(key_of[2], (VALUE_FEATURES,), 0.5, 3.0, ((0, 4),), jnp.float32)
    adapter_down_factors = gaussian(own_keys[3], (ADAPTER_COUNT, ADAPTER_RANK, MODEL_WIDTH), MODEL_WIDTH ** -0.5, 0.0625, ((0, 4), (2, 4)))
    adapter_up_factors = gaussian(own_keys[4], (ADAPTER_COUNT, ADAPTER_RANK, VALUE_FEATURES), ADAPTER_RANK ** -0.5, 0.75, ((0, 4),))
    adapter_replica_keys = jax.random.split(jax.random.fold_in(own_keys[5], 1), REQUEST_COUNT // R_DEV)
    adapter_replica_turns = jax.random.permutation(jax.random.fold_in(own_keys[5], 3), REQUEST_COUNT // R_DEV)
    adapter_replica = jax.vmap(lambda own, number: assign_block(jax.random.fold_in(own_keys[5], 2), own, number, R_DEV, N_REPLICA, 1, CAP, 2))(adapter_replica_keys, adapter_replica_turns).reshape((REQUEST_COUNT, 1))
    adapter_position = with_ends(jax.random.randint(own_keys[6], (REQUEST_COUNT,), 0, ADP_DEV), jax.random.fold_in(own_keys[6], 1), 0, ADP_DEV - 1).astype(jnp.int32)
    queries = draw_queries(jax.random.fold_in(jax.random.fold_in(key_of[12], part), 71), part)
    cached_key_rows = draw_cached_key_rows(jax.random.fold_in(jax.random.fold_in(key_of[12], part), 71), part)
    cached_value_rows = gaussian(own_keys[9], (REQUEST_COUNT, KEY_HEADS, LEN, HEAD_WIDTH), 1.0, 6.0, ((0, 4), (1, 4)))
    incoming_keys = gaussian(own_keys[10], (REQUEST_COUNT, KEY_HEADS, HEAD_WIDTH), 1.0, 6.0, ((0, 4), (1, 4)))
    lengths = draw_lengths(jax.random.fold_in(jax.random.fold_in(key_of[12], part), 71), part)
    return {"activations": activations, "value_matrix": value_matrix, "value_offset_bias": value_offset_bias, "adapter_down_factors": adapter_down_factors, "adapter_up_factors": adapter_up_factors, "adapter_replica": adapter_replica, "adapter_position": adapter_position, "queries": queries, "cached_key_rows": cached_key_rows, "cached_value_rows": cached_value_rows, "incoming_keys": incoming_keys, "lengths": lengths}


adapter_scale = 0.5


def reference(activations, value_matrix, value_offset_bias, adapter_down_factors, adapter_up_factors, adapter_replica, adapter_position, queries, cached_key_rows, cached_value_rows, incoming_keys, lengths):
    adapter = (adapter_replica[:, 0] * ADP_DEV + adapter_position).astype(jnp.int32)
    base_output = jnp.dot(activations, value_matrix, preferred_element_type=jnp.float32)

    def one_block(operands):
        block_rows, block_indices = operands
        down_selected = adapter_down_factors[block_indices].astype(jnp.float32)
        up_selected = adapter_up_factors[block_indices].astype(jnp.float32)
        rank_vec = jnp.einsum("rd,rkd->rk", block_rows.astype(jnp.float32), down_selected, precision=lax.Precision.HIGHEST)
        return jnp.einsum("rk,rkc->rc", rank_vec, up_selected, precision=lax.Precision.HIGHEST)

    adapter_delta = lax.map(one_block, (activations.reshape(REQUEST_COUNT // 8, 8, MODEL_WIDTH), adapter.reshape(REQUEST_COUNT // 8, 8)))
    adapter_delta = adapter_delta.reshape(REQUEST_COUNT, VALUE_FEATURES)
    incoming_values = (base_output + value_offset_bias + adapter_scale * adapter_delta).astype(jnp.bfloat16).reshape(REQUEST_COUNT, KEY_HEADS, HEAD_WIDTH)

    group_size = QH // KEY_HEADS
    score_scale = 1.0 / (HEAD_WIDTH ** 0.5)
    query_blocks = queries.reshape(REQUEST_COUNT, KEY_HEADS, group_size, HEAD_WIDTH).astype(jnp.float32)
    cached = jnp.einsum("rhgd,rhld->rhgl", query_blocks, cached_key_rows.astype(jnp.float32), precision=lax.Precision.HIGHEST) * score_scale
    valid_slots = jnp.arange(LEN)[None, :] < lengths[:, None]
    cached = jnp.where(valid_slots[:, None, None, :], cached, -1e30)
    fresh_score = jnp.einsum("rhgd,rhd->rhg", query_blocks, incoming_keys.astype(jnp.float32), precision=lax.Precision.HIGHEST) * score_scale
    row_max = jnp.maximum(jnp.max(cached, axis=-1), fresh_score)
    weights_cached = jnp.exp(cached - row_max[..., None])
    weights_fresh = jnp.exp(fresh_score - row_max)
    row_total = jnp.sum(weights_cached, axis=-1) + weights_fresh
    probs_cached = (weights_cached / row_total[..., None]).astype(jnp.bfloat16)
    probs_fresh = (weights_fresh / row_total).astype(jnp.bfloat16)
    context = jnp.einsum("rhgl,rhld->rhgd", probs_cached.astype(jnp.float32), cached_value_rows.astype(jnp.float32), precision=lax.Precision.HIGHEST)
    context = context + jnp.einsum("rhg,rhd->rhgd", probs_fresh.astype(jnp.float32), incoming_values.astype(jnp.float32), precision=lax.Precision.HIGHEST)
    context = context.reshape(REQUEST_COUNT, QH, HEAD_WIDTH).astype(jnp.bfloat16)
    return context, incoming_values
```

```python
import functools

import jax
import jax.numpy as jnp
from jax import lax
from jax.experimental import pallas as pl
from jax.experimental.pallas import tpu as pltpu
from jax.sharding import PartitionSpec as P

adapter_scale = 0.5
lanes = 128
f32 = jnp.float32
bf16 = jnp.bfloat16
VMEM = pl.BlockSpec(memory_space=pltpu.VMEM)


def call(kernel, name, outs, args, flops, limit=32 << 20, **more):
    read = sum(a.size * a.dtype.itemsize for a in args)
    write = sum(o.size * o.dtype.itemsize for o in outs)
    return pl.pallas_call(
        kernel,
        name=name,
        out_shape=outs,
        cost_estimate=pl.CostEstimate(flops=flops, bytes_accessed=read + write, transcendentals=0),
        compiler_params=pltpu.CompilerParams(vmem_limit_bytes=limit),
        **more,
    )(*args)


def struct(shape, dtype):
    return jax.ShapeDtypeStruct(shape, dtype)


def placement(home_ref, blocks, capacity, relative):
    home = home_ref[...]
    rows = home.shape[0]
    if relative:
        home = home ^ lax.axis_index("replica")
    hot = (home == lax.broadcasted_iota(jnp.int32, (rows, blocks), 1)).astype(f32)
    row = lax.broadcasted_iota(jnp.int32, (rows, rows), 0)
    column = lax.broadcasted_iota(jnp.int32, (rows, rows), 1)
    below = (column < row).astype(bf16)
    before = jnp.dot(below, hot.astype(bf16), preferred_element_type=f32)
    position = jnp.sum(before * hot, axis=1, keepdims=True).astype(jnp.int32)
    flat = home * capacity + position
    return flat == lax.broadcasted_iota(jnp.int32, (rows, blocks * capacity), 1)


def pack_kernel(blocks, capacity, relative, home_ref, slot_ref, rows_ref, *outs):
    place = placement(home_ref, blocks, capacity, relative)
    rows, width = rows_ref.shape
    square = lax.broadcasted_iota(jnp.int32, (rows, rows), 0) == lax.broadcasted_iota(
        jnp.int32, (rows, rows), 1
    )
    slot = jnp.sum(jnp.where(square, slot_ref[...], 0), axis=1, keepdims=True) + 1
    spread = jnp.broadcast_to(slot.astype(f32), (rows, lanes)).astype(bf16)
    turned = place.astype(f32).astype(bf16)
    over = (((0,), (0,)), ((), ()))
    packed = lax.dot_general(turned, rows_ref[...], over, preferred_element_type=f32).astype(bf16)
    slots = lax.dot_general(turned, spread, over, preferred_element_type=f32).astype(bf16)
    size = outs[0].shape[0]
    for b, out in enumerate(outs):
        out[:, :width] = packed[b * size : (b + 1) * size]
        out[:, width:] = slots[b * size : (b + 1) * size]


def rank_kernel(pieces, adapters, *refs):
    got = refs[:pieces]
    down_ref, base_ref, rank_ref, slot_ref = refs[pieces : pieces + 4]
    messages = refs[pieces + 4 :]
    features = down_ref.shape[1]
    rows = jnp.concatenate([ref[:, :features] for ref in got], axis=0)
    slots = jnp.concatenate([ref[:, features:] for ref in got], axis=0).astype(f32)
    slot_ref[...] = slots
    across = (((1,), (1,)), ((), ()))
    projected = lax.dot_general(rows, down_ref[...], across, preferred_element_type=f32)
    width = down_ref.shape[0] // adapters
    total = None
    for a in range(adapters):
        term = projected[:, a * width : (a + 1) * width]
        term = jnp.where(slots[:, :width] == a + 1.0, term, 0.0)
        total = term if total is None else total + term
    rank_ref[...] = total
    upper = total.astype(bf16)
    lower = (total - upper.astype(f32)).astype(bf16)
    pair = jnp.concatenate([upper, lower], axis=1)
    me = lax.axis_index("tensor")
    for d, message in enumerate(messages):
        block = base_ref[me ^ (d + 1)].astype(bf16)
        at = 0
        for c in range(block.shape[1] // lanes):
            message[at : at + block.shape[0], :] = block[:, c * lanes : (c + 1) * lanes]
            at += block.shape[0]
        message[at:, :] = pair


def up_kernel(peers, adapters, *refs):
    got = refs[:peers]
    rank_ref, slot_ref, up_ref = refs[peers : peers + 3]
    outs = refs[peers + 3 :]
    total = rank_ref[...]
    count, width = total.shape
    for ref in got:
        pair = ref[ref.shape[0] - count :, :].astype(f32)
        total = total + (pair[:, :width] + pair[:, width:])
    slots = slot_ref[:, :width]
    wide = jnp.concatenate(
        [jnp.where(slots == a + 1.0, total, 0.0) for a in range(adapters)], axis=1
    )
    upper = wide.astype(bf16)
    lower = (wide - upper.astype(f32)).astype(bf16)
    term = jnp.dot(upper, up_ref[...], preferred_element_type=f32)
    term = adapter_scale * (term + jnp.dot(lower, up_ref[...], preferred_element_type=f32))
    term = term.astype(bf16)
    size = outs[0].shape[0]
    for b, out in enumerate(outs):
        out[...] = term[b * size : (b + 1) * size]


def sum_kernel(peers, *refs):
    got = refs[:peers]
    base_ref, bias_ref, out = refs[peers:]
    total = base_ref[lax.axis_index("tensor")] + bias_ref[...]
    rows = total.shape[0]
    for c in range(total.shape[1] // lanes):
        part = total[:, c * lanes : (c + 1) * lanes]
        for ref in got:
            part = part + ref[c * rows : (c + 1) * rows, :].astype(f32)
        out[:, c * lanes : (c + 1) * lanes] = part


def last_kernel(pieces, blocks, capacity, relative, *refs):
    got = refs[:pieces]
    home_ref, base_ref, cached_ref, fresh_ref, context_ref, values_ref = refs[pieces:]
    place = placement(home_ref, blocks, capacity, relative).astype(f32).astype(bf16)
    terms = jnp.concatenate([ref[...] for ref in got], axis=0)
    picked = jnp.dot(place, terms, preferred_element_type=f32)
    values = (base_ref[...] + picked).astype(bf16)
    heads, size = values_ref.shape[1:]
    group = cached_ref.shape[1] // heads
    for h in range(heads):
        value = values[:, h * size : (h + 1) * size].astype(f32)
        values_ref[:, h, :] = value.astype(bf16)
        own = slice(h * group, (h + 1) * group)
        context = cached_ref[:, own, :] + fresh_ref[:, own, :] * value[:, None, :]
        context_ref[:, own, :] = context.astype(bf16)


def base_kernel(rows_ref, matrix_ref, out):
    parts, _, width = out.shape
    product = jnp.dot(rows_ref[...], matrix_ref[...], preferred_element_type=f32)

    @pl.when(pl.program_id(0) == 0)
    def _():
        for t in range(parts):
            out[t] = product[:, t * width : (t + 1) * width]

    @pl.when(pl.program_id(0) > 0)
    def _():
        for t in range(parts):
            out[t] += product[:, t * width : (t + 1) * width]


def attention_kernel(length_ref, query_ref, key_ref, value_ref, new_ref, cached_ref, fresh_ref):
    requests, heads, length, size = key_ref.shape
    group = query_ref.shape[1] // heads
    scale = 1.0 / size**0.5
    step = pl.program_id(0)
    slot = lax.broadcasted_iota(jnp.int32, (group, length), 1)
    for r in range(requests):
        valid = slot < length_ref[step * requests + r]
        for h in range(heads):
            own = slice(h * group, (h + 1) * group)
            query = query_ref[r, own, :]
            across = (((1,), (1,)), ((), ()))
            scores = lax.dot_general(query, key_ref[r, h], across, preferred_element_type=f32)
            scores = jnp.where(valid, scores * scale, -1e30)
            new = new_ref[r, h : h + 1, :].astype(f32)
            fresh = jnp.sum(query.astype(f32) * new, axis=1, keepdims=True) * scale
            top = jnp.maximum(jnp.max(scores, axis=1, keepdims=True), fresh)
            weights = jnp.exp(scores - top)
            alone = jnp.exp(fresh - top)
            total = jnp.sum(weights, axis=1, keepdims=True) + alone
            probs = (weights / total).astype(bf16)
            cached_ref[r, own, :] = jnp.dot(probs, value_ref[r, h], preferred_element_type=f32)
            share = jnp.broadcast_to(alone / total, (group, size))
            fresh_ref[r, own, :] = share.astype(bf16).astype(f32)


def attention(lengths, queries, keys, values, new_keys):
    rows, heads, length, size = keys.shape
    query_heads = queries.shape[1]
    steps = 4
    part = rows // steps
    shape = (rows, query_heads, size)
    q_spec = pl.BlockSpec((part, query_heads, size), lambda i, _: (i, 0, 0))
    kv_spec = pl.BlockSpec((part, heads, length, size), lambda i, _: (i, 0, 0, 0))
    n_spec = pl.BlockSpec((part, heads, size), lambda i, _: (i, 0, 0))
    return call(
        attention_kernel,
        "attention",
        [struct(shape, f32), struct(shape, f32)],
        [lengths, queries, keys, values, new_keys],
        4 * rows * query_heads * length * size,
        grid_spec=pltpu.PrefetchScalarGridSpec(
            num_scalar_prefetch=1,
            grid=(steps,),
            in_specs=[q_spec, kv_spec, kv_spec, n_spec],
            out_specs=[q_spec, q_spec],
        ),
    )


def base_product(rows, matrix, parts):
    count, depth = rows.shape
    width = matrix.shape[1] // parts
    steps = 4
    return call(
        base_kernel,
        "base",
        [struct((parts, count, width), f32)],
        [rows, matrix],
        2 * count * depth * matrix.shape[1],
        grid=(steps,),
        in_specs=[
            pl.BlockSpec((count, depth // steps), lambda i: (0, i)),
            pl.BlockSpec((depth // steps, matrix.shape[1]), lambda i: (i, 0)),
        ],
        out_specs=[pl.BlockSpec((parts, count, width), lambda i: (0, 0, 0))],
    )[0]


def exchange(blocks, axis):
    size = lax.axis_size(axis)
    got = [
        lax.ppermute(block, axis, [(i, i ^ (d + 1)) for i in range(size)])
        for d, block in enumerate(blocks[1:])
    ]
    return [blocks[0]] + got


def per_device(
    activations,
    value_matrix,
    value_offset_bias,
    adapter_down_factors,
    adapter_up_factors,
    adapter_replica,
    adapter_position,
    queries,
    cached_key_rows,
    cached_value_rows,
    incoming_keys,
    lengths,
):
    rows, features = activations.shape
    replicas = lax.axis_size("replica")
    parts = lax.axis_size("tensor")
    capacity = max(2, 2 * rows // replicas)
    adapters, rank, _ = adapter_down_factors.shape
    width = value_matrix.shape[1] // parts
    heads, size = incoming_keys.shape[1:]
    slots = replicas * capacity
    direct = capacity % 16 == 0

    def move(blocks):
        if direct:
            return exchange(blocks, "replica")
        block = blocks[0].reshape(replicas, capacity, -1)
        block = lax.all_to_all(block, "replica", split_axis=0, concat_axis=0, tiled=True)
        return [block.reshape(slots, -1)]

    pieces = replicas if direct else 1
    piece = slots // pieces
    packed = call(
        functools.partial(pack_kernel, replicas, capacity, direct),
        "pack",
        [struct((piece, features + lanes), bf16)] * pieces,
        [adapter_replica, adapter_position.reshape(1, rows), activations],
        2 * rows * slots * features,
        in_specs=[VMEM] * 3,
        out_specs=[VMEM] * pieces,
    )
    got = move(packed)
    base = base_product(activations, value_matrix, parts)
    cached, fresh = attention(
        lengths, queries, cached_key_rows, cached_value_rows, incoming_keys
    )
    long = rows * (width // lanes) + slots
    rank_own, slot_ids, *messages = call(
        functools.partial(rank_kernel, pieces, adapters),
        "rank",
        [struct((slots, rank), f32), struct((slots, lanes), f32)]
        + [struct((long, lanes), bf16)] * (parts - 1),
        [*got, adapter_down_factors.reshape(adapters * rank, features), base],
        2 * slots * adapters * rank * features,
        in_specs=[VMEM] * (pieces + 2),
        out_specs=[VMEM] * (parts + 1),
    )
    heard = exchange([None, *messages], "tensor")[1:]
    up_local = lax.dynamic_slice_in_dim(
        adapter_up_factors, lax.axis_index("tensor") * width, width, 2
    ).reshape(adapters * rank, width)
    terms = call(
        functools.partial(up_kernel, parts - 1, adapters),
        "up",
        [struct((piece, width), bf16)] * pieces,
        [*heard, rank_own, slot_ids, up_local],
        4 * slots * adapters * rank * width,
        in_specs=[VMEM] * (parts + 2),
        out_specs=[VMEM] * pieces,
    )
    returned = move(terms)
    total = call(
        functools.partial(sum_kernel, parts - 1),
        "base_sum",
        [struct((rows, width), f32)],
        [*heard, base, value_offset_bias.reshape(1, width)],
        parts * rows * width,
        in_specs=[VMEM] * (parts + 1),
        out_specs=[VMEM],
    )[0]
    context, values = call(
        functools.partial(last_kernel, pieces, replicas, capacity, direct),
        "last",
        [struct(queries.shape, bf16), struct((rows, heads, size), bf16)],
        [*returned, adapter_replica, total, cached, fresh],
        2 * rows * slots * width,
        in_specs=[VMEM] * (pieces + 4),
        out_specs=[VMEM] * 2,
    )
    return (context, values)


def solution(mesh):
    rows = P(("groups", "replica"))
    split = P(("groups", "replica"), "tensor")
    in_specs = (
        split,
        P("tensor", None),
        P("tensor"),
        P(("groups", "replica"), None, "tensor"),
        rows,
        rows,
        rows,
        split,
        split,
        split,
        split,
        rows,
    )
    return jax.shard_map(
        per_device, mesh=mesh, in_specs=in_specs, out_specs=(split, split), check_vma=False
    )
```

```python
import functools

import jax
import jax.numpy as jnp
from jax import lax
from jax.experimental import pallas as pl
from jax.experimental.pallas import tpu as pltpu
from jax.sharding import PartitionSpec as P

adapter_scale = 0.5
lanes = 128
f32 = jnp.float32
bf16 = jnp.bfloat16
VMEM = pl.BlockSpec(memory_space=pltpu.VMEM)
HBM = pl.BlockSpec(memory_space=pltpu.HBM)


def call(kernel, name, outs, args, flops, limit=16 << 20, **more):
    read = sum(a.size * a.dtype.itemsize for a in args)
    write = sum(o.size * o.dtype.itemsize for o in outs)
    return pl.pallas_call(
        kernel,
        name=name,
        out_shape=outs,
        cost_estimate=pl.CostEstimate(flops=flops, bytes_accessed=read + write, transcendentals=0),
        compiler_params=pltpu.CompilerParams(vmem_limit_bytes=limit),
        **more,
    )(*args)


def stay(array):
    return pltpu.with_memory_space_constraint(array, pltpu.HBM)


def struct(shape, dtype):
    return jax.ShapeDtypeStruct(shape, dtype)


def column(row):
    count = row.shape[1]
    square = lax.broadcasted_iota(jnp.int32, (count, count), 0) == lax.broadcasted_iota(
        jnp.int32, (count, count), 1
    )
    return jnp.sum(jnp.where(square, row, 0), axis=1, keepdims=True)


def placement(home_row, blocks, capacity, relative):
    home = column(home_row)
    rows = home.shape[0]
    if relative:
        home = home ^ lax.axis_index("replica")
    hot = (home == lax.broadcasted_iota(jnp.int32, (rows, blocks), 1)).astype(f32)
    at = lax.broadcasted_iota(jnp.int32, (rows, rows), 0)
    below = (lax.broadcasted_iota(jnp.int32, (rows, rows), 1) < at).astype(bf16)
    before = jnp.dot(below, hot.astype(bf16), preferred_element_type=f32)
    position = jnp.sum(before * hot, axis=1, keepdims=True).astype(jnp.int32)
    flat = home * capacity + position
    return flat == lax.broadcasted_iota(jnp.int32, (rows, blocks * capacity), 1)


def pack_kernel(blocks, capacity, relative, home_hbm, slot_hbm, rows_hbm, rows_ref, *refs):
    outs, (home_ref, slot_ref, semaphores) = refs[:-3], refs[-3:]
    copies = [
        pltpu.make_async_copy(source, target, semaphores.at[i])
        for i, (source, target) in enumerate(
            [(home_hbm, home_ref), (slot_hbm, slot_ref), (rows_hbm, rows_ref)]
        )
    ]
    for copy in copies:
        copy.start()
    copies[0].wait()
    place = placement(home_ref[...], blocks, capacity, relative)
    rows, width = rows_ref.shape
    copies[1].wait()
    slot = (column(slot_ref[...]) + 1).astype(f32)
    spread = jnp.broadcast_to(slot, (rows, lanes)).astype(bf16)
    turned = place.astype(f32).astype(bf16)
    over = (((0,), (0,)), ((), ()))
    slots = lax.dot_general(turned, spread, over, preferred_element_type=f32).astype(bf16)
    copies[2].wait()
    packed = lax.dot_general(turned, rows_ref[...], over, preferred_element_type=f32).astype(bf16)
    size = outs[0].shape[0]
    for b, out in enumerate(outs):
        out[:, :width] = packed[b * size : (b + 1) * size]
        out[:, width:] = slots[b * size : (b + 1) * size]


def rank_kernel(pieces, adapters, *refs):
    got = refs[:pieces]
    down_ref, base_ref, rank_ref, slot_ref = refs[pieces : pieces + 4]
    messages = refs[pieces + 4 :]
    features = down_ref.shape[1]
    rows = jnp.concatenate([ref[:, :features] for ref in got], axis=0)
    slots = jnp.concatenate([ref[:, features:] for ref in got], axis=0).astype(f32)
    slot_ref[...] = slots
    across = (((1,), (1,)), ((), ()))
    projected = lax.dot_general(rows, down_ref[...], across, preferred_element_type=f32)
    width = down_ref.shape[0] // adapters
    total = None
    for a in range(adapters):
        term = projected[:, a * width : (a + 1) * width]
        term = jnp.where(slots[:, :width] == a + 1.0, term, 0.0)
        total = term if total is None else total + term
    rank_ref[...] = total
    upper = total.astype(bf16)
    lower = (total - upper.astype(f32)).astype(bf16)
    pair = jnp.concatenate([upper, lower], axis=1)
    me = lax.axis_index("tensor")
    for d, message in enumerate(messages):
        block = base_ref[me ^ (d + 1)].astype(bf16)
        at = 0
        for c in range(block.shape[1] // lanes):
            message[at : at + block.shape[0], :] = block[:, c * lanes : (c + 1) * lanes]
            at += block.shape[0]
        message[at:, :] = pair


def up_kernel(peers, adapters, *refs):
    got = refs[:peers]
    rank_ref, slot_ref, up_ref = refs[peers : peers + 3]
    outs = refs[peers + 3 :]
    total = rank_ref[...]
    count, width = total.shape
    for ref in got:
        pair = ref[ref.shape[0] - count :, :].astype(f32)
        total = total + (pair[:, :width] + pair[:, width:])
    slots = slot_ref[:, :width]
    wide = jnp.concatenate(
        [jnp.where(slots == a + 1.0, total, 0.0) for a in range(adapters)], axis=1
    )
    upper = wide.astype(bf16)
    lower = (wide - upper.astype(f32)).astype(bf16)
    term = jnp.dot(upper, up_ref[...], preferred_element_type=f32)
    term = adapter_scale * (term + jnp.dot(lower, up_ref[...], preferred_element_type=f32))
    term = term.astype(bf16)
    size = outs[0].shape[0]
    for b, out in enumerate(outs):
        out[...] = term[b * size : (b + 1) * size]


def sum_kernel(peers, *refs):
    got = refs[:peers]
    base_ref, bias_ref, out = refs[peers:]
    total = base_ref[lax.axis_index("tensor")] + bias_ref[...]
    rows = total.shape[0]
    for c in range(total.shape[1] // lanes):
        part = total[:, c * lanes : (c + 1) * lanes]
        for ref in got:
            part = part + ref[c * rows : (c + 1) * rows, :].astype(f32)
        out[:, c * lanes : (c + 1) * lanes] = part


def last_kernel(pieces, blocks, capacity, relative, *refs):
    got = refs[:pieces]
    home_ref, base_ref, cached_ref, fresh_ref, context_ref, values_ref = refs[pieces:]
    place = placement(home_ref[...], blocks, capacity, relative).astype(f32).astype(bf16)
    terms = jnp.concatenate([ref[...] for ref in got], axis=0)
    picked = jnp.dot(place, terms, preferred_element_type=f32)
    values = (base_ref[...] + picked).astype(bf16)
    heads, size = values_ref.shape[1:]
    group = cached_ref.shape[1] // heads
    for h in range(heads):
        value = values[:, h * size : (h + 1) * size].astype(f32)
        values_ref[:, h, :] = value.astype(bf16)
        own = slice(h * group, (h + 1) * group)
        context = cached_ref[:, own, :] + fresh_ref[:, own, :] * value[:, None, :]
        context_ref[:, own, :] = context.astype(bf16)


def base_kernel(rows_ref, matrix_ref, out):
    parts, _, width = out.shape
    for t in range(parts):
        block = matrix_ref[:, t * width : (t + 1) * width]
        out[t] = jnp.dot(rows_ref[...], block, preferred_element_type=f32)


def base_product(rows, matrix, parts):
    count, depth = rows.shape
    width = matrix.shape[1] // parts
    return call(
        base_kernel,
        "base",
        [struct((parts, count, width), f32)],
        [rows, matrix],
        2 * count * depth * matrix.shape[1],
        in_specs=[VMEM] * 2,
        out_specs=[VMEM],
    )[0]


def attention_kernel(
    length_ref, query_ref, key_ref, value_ref, new_ref, cached_ref, fresh_ref, score_ref, prob_ref
):
    requests, heads, length, size = key_ref.shape
    group = query_ref.shape[1] // heads
    scale = 1.0 / size**0.5
    count = requests * heads
    across = (((1,), (1,)), ((), ()))
    pairs = [(r, h) for r in range(requests) for h in range(heads)]
    for i, (r, h) in enumerate(pairs):
        query = query_ref[r, h * group : (h + 1) * group, :]
        score_ref[i] = lax.dot_general(query, key_ref[r, h], across, preferred_element_type=f32)
    filled = jnp.concatenate(
        [jnp.full((heads, 1, length), length_ref[r], jnp.int32) for r in range(requests)], axis=0
    )
    valid = lax.broadcasted_iota(jnp.int32, (count, group, length), 2) < filled
    scores = jnp.where(valid, score_ref[...] * scale, -1e30)
    query = query_ref[...].reshape(count, group, size).astype(f32)
    new = new_ref[...].astype(f32).reshape(count, 1, size)
    fresh = jnp.sum(query * new, axis=2, keepdims=True) * scale
    top = jnp.maximum(jnp.max(scores, axis=2, keepdims=True), fresh)
    weights = jnp.exp(scores - top)
    alone = jnp.exp(fresh - top)
    total = jnp.sum(weights, axis=2, keepdims=True) + alone
    prob_ref[...] = (weights / total).astype(bf16)
    share = jnp.broadcast_to((alone / total).astype(bf16).astype(f32), (count, group, size))
    fresh_ref[...] = share.reshape(requests, heads * group, size)
    for i, (r, h) in enumerate(pairs):
        own = slice(h * group, (h + 1) * group)
        cached_ref[r, own, :] = jnp.dot(prob_ref[i], value_ref[r, h], preferred_element_type=f32)


def attention(lengths, queries, keys, values, new_keys):
    rows, heads, length, size = keys.shape
    query_heads = queries.shape[1]
    group = query_heads // heads
    shape = struct((rows, query_heads, size), f32)
    return call(
        attention_kernel,
        "attention",
        [shape, shape],
        [lengths, queries, keys, values, new_keys],
        4 * rows * query_heads * length * size,
        in_specs=[pl.BlockSpec(memory_space=pltpu.SMEM)] + [VMEM] * 4,
        out_specs=[VMEM] * 2,
        scratch_shapes=[
            pltpu.VMEM((rows * heads, group, length), f32),
            pltpu.VMEM((rows * heads, group, length), bf16),
        ],
    )


def exchange(blocks, axis):
    size = lax.axis_size(axis)
    got = [
        lax.ppermute(block, axis, [(i, i ^ (d + 1)) for i in range(size)])
        for d, block in enumerate(blocks[1:])
    ]
    return [blocks[0]] + got


def per_device(
    activations,
    value_matrix,
    value_offset_bias,
    adapter_down_factors,
    adapter_up_factors,
    adapter_replica,
    adapter_position,
    queries,
    cached_key_rows,
    cached_value_rows,
    incoming_keys,
    lengths,
):
    rows, features = activations.shape
    replicas = lax.axis_size("replica")
    parts = lax.axis_size("tensor")
    capacity = max(2, 2 * rows // replicas)
    adapters, rank, _ = adapter_down_factors.shape
    width = value_matrix.shape[1] // parts
    heads, size = incoming_keys.shape[1:]
    slots = replicas * capacity
    direct = capacity % 16 == 0
    home_row = adapter_replica.reshape(1, rows)

    def move(blocks):
        if direct:
            return exchange(blocks, "replica")
        block = blocks[0].reshape(replicas, capacity, -1)
        block = lax.all_to_all(block, "replica", split_axis=0, concat_axis=0, tiled=True)
        return [block.reshape(slots, -1)]

    pieces = replicas if direct else 1
    piece = slots // pieces
    local_rows, *packed = call(
        functools.partial(pack_kernel, replicas, capacity, direct),
        "pack",
        [struct(activations.shape, bf16)] + [struct((piece, features + lanes), bf16)] * pieces,
        [stay(home_row), stay(adapter_position.reshape(1, rows)), stay(activations)],
        4_000_000_000,
        in_specs=[HBM] * 3,
        out_specs=[VMEM] * (pieces + 1),
        scratch_shapes=[
            pltpu.VMEM((1, rows), jnp.int32),
            pltpu.VMEM((1, rows), jnp.int32),
            pltpu.SemaphoreType.DMA((3,)),
        ],
    )
    got = move(packed)
    base = base_product(local_rows, value_matrix, parts)
    cached, fresh = attention(
        lengths, queries, cached_key_rows, cached_value_rows, incoming_keys
    )
    base, cached, fresh = lax.optimization_barrier((base, cached, fresh))
    long = rows * (width // lanes) + slots
    rank_own, slot_ids, *messages = call(
        functools.partial(rank_kernel, pieces, adapters),
        "rank",
        [struct((slots, rank), f32), struct((slots, lanes), f32)]
        + [struct((long, lanes), bf16)] * (parts - 1),
        [*got, adapter_down_factors.reshape(adapters * rank, features), base],
        2 * slots * adapters * rank * features,
        in_specs=[VMEM] * (pieces + 2),
        out_specs=[VMEM] * (parts + 1),
    )
    heard = exchange([None, *messages], "tensor")[1:]
    up_local = lax.dynamic_slice_in_dim(
        adapter_up_factors, lax.axis_index("tensor") * width, width, 2
    ).reshape(adapters * rank, width)
    terms = call(
        functools.partial(up_kernel, parts - 1, adapters),
        "up",
        [struct((piece, width), bf16)] * pieces,
        [*heard, rank_own, slot_ids, up_local],
        4 * slots * adapters * rank * width,
        in_specs=[VMEM] * (parts + 2),
        out_specs=[VMEM] * pieces,
    )
    returned = move(terms)
    total = call(
        functools.partial(sum_kernel, parts - 1),
        "base_sum",
        [struct((rows, width), f32)],
        [*heard, base, value_offset_bias.reshape(1, width)],
        parts * rows * width,
        in_specs=[VMEM] * (parts + 1),
        out_specs=[VMEM],
    )[0]
    context, values = call(
        functools.partial(last_kernel, pieces, replicas, capacity, direct),
        "last",
        [struct(queries.shape, bf16), struct((rows, heads, size), bf16)],
        [*returned, home_row, total, cached, fresh],
        2 * rows * slots * width,
        in_specs=[VMEM] * (pieces + 4),
        out_specs=[VMEM] * 2,
    )
    return (context, values)


def solution(mesh):
    rows = P(("groups", "replica"))
    split = P(("groups", "replica"), "tensor")
    in_specs = (
        split,
        P("tensor", None),
        P("tensor"),
        P(("groups", "replica"), None, "tensor"),
        rows,
        rows,
        rows,
        split,
        split,
        split,
        split,
        rows,
    )
    return jax.shard_map(
        per_device, mesh=mesh, in_specs=in_specs, out_specs=(split, split), check_vma=False
    )
```

```python
import functools

import jax
import jax.numpy as jnp
from jax import lax
from jax.experimental import pallas as pl
from jax.experimental.pallas import tpu as pltpu
from jax.sharding import PartitionSpec as P

adapter_scale = 0.5
pack_cost = 40_000_000_000
lanes = 128
f32 = jnp.float32
bf16 = jnp.bfloat16
VMEM = pl.BlockSpec(memory_space=pltpu.VMEM)
HBM = pl.BlockSpec(memory_space=pltpu.HBM)


def call(kernel, name, outs, args, flops, limit=16 << 20, **more):
    read = sum(a.size * a.dtype.itemsize for a in args)
    write = sum(o.size * o.dtype.itemsize for o in outs)
    return pl.pallas_call(
        kernel,
        name=name,
        out_shape=outs,
        cost_estimate=pl.CostEstimate(flops=flops, bytes_accessed=read + write, transcendentals=0),
        compiler_params=pltpu.CompilerParams(vmem_limit_bytes=limit),
        **more,
    )(*args)


def stay(array):
    return pltpu.with_memory_space_constraint(array, pltpu.HBM)


def struct(shape, dtype):
    return jax.ShapeDtypeStruct(shape, dtype)


def column(row):
    count = row.shape[1]
    square = lax.broadcasted_iota(jnp.int32, (count, count), 0) == lax.broadcasted_iota(
        jnp.int32, (count, count), 1
    )
    return jnp.sum(jnp.where(square, row, 0), axis=1, keepdims=True)


def orders(blocks):
    if blocks == 4:
        return [0, 2, 1, 3], [0, 2, 1, 3]
    return list(range(blocks)), list(range(blocks))


def placement(home_row, blocks, capacity, relative, ordered):
    home = column(home_row)
    rows = home.shape[0]
    if relative:
        step = home ^ lax.axis_index("replica")
        home = step
        if ordered:
            odd = lax.axis_index("tensor") % 2 == 1
            for at, (a, b) in enumerate(zip(*orders(blocks))):
                home = jnp.where(step == jnp.where(odd, b, a), at, home)
    hot = (home == lax.broadcasted_iota(jnp.int32, (rows, blocks), 1)).astype(f32)
    at = lax.broadcasted_iota(jnp.int32, (rows, rows), 0)
    below = (lax.broadcasted_iota(jnp.int32, (rows, rows), 1) < at).astype(bf16)
    before = jnp.dot(below, hot.astype(bf16), preferred_element_type=f32)
    position = jnp.sum(before * hot, axis=1, keepdims=True).astype(jnp.int32)
    flat = home * capacity + position
    return flat == lax.broadcasted_iota(jnp.int32, (rows, blocks * capacity), 1)


def pack_kernel(blocks, capacity, relative, home_hbm, slot_hbm, rows_hbm, rows_ref, *refs):
    outs, (home_ref, slot_ref, semaphores) = refs[:-3], refs[-3:]
    copies = [
        pltpu.make_async_copy(source, target, semaphores.at[i])
        for i, (source, target) in enumerate(
            [(home_hbm, home_ref), (slot_hbm, slot_ref), (rows_hbm, rows_ref)]
        )
    ]
    for copy in copies:
        copy.start()
    copies[0].wait()
    place = placement(home_ref[...], blocks, capacity, relative, True)
    rows, width = rows_ref.shape
    copies[1].wait()
    slot = (column(slot_ref[...]) + 1).astype(f32)
    spread = jnp.broadcast_to(slot, (rows, lanes)).astype(bf16)
    turned = place.astype(f32).astype(bf16)
    over = (((0,), (0,)), ((), ()))
    slots = lax.dot_general(turned, spread, over, preferred_element_type=f32).astype(bf16)
    copies[2].wait()
    packed = lax.dot_general(turned, rows_ref[...], over, preferred_element_type=f32).astype(bf16)
    size = outs[0].shape[0]
    for b, out in enumerate(outs):
        out[:, :width] = packed[b * size : (b + 1) * size]
        out[:, width:] = slots[b * size : (b + 1) * size]


def rank_kernel(pieces, adapters, *refs):
    got = refs[:pieces]
    down_ref, base_ref, rank_ref, slot_ref = refs[pieces : pieces + 4]
    messages = refs[pieces + 4 :]
    features = down_ref.shape[1]
    rows = jnp.concatenate([ref[:, :features] for ref in got], axis=0)
    slots = jnp.concatenate([ref[:, features:] for ref in got], axis=0).astype(f32)
    slot_ref[...] = slots
    across = (((1,), (1,)), ((), ()))
    projected = lax.dot_general(rows, down_ref[...], across, preferred_element_type=f32)
    width = down_ref.shape[0] // adapters
    total = None
    for a in range(adapters):
        term = projected[:, a * width : (a + 1) * width]
        term = jnp.where(slots[:, :width] == a + 1.0, term, 0.0)
        total = term if total is None else total + term
    rank_ref[...] = total
    upper = total.astype(bf16)
    lower = (total - upper.astype(f32)).astype(bf16)
    pair = jnp.concatenate([upper, lower], axis=1)
    me = lax.axis_index("tensor")
    for d, message in enumerate(messages):
        block = base_ref[me ^ (d + 1)].astype(bf16)
        at = 0
        for c in range(block.shape[1] // lanes):
            message[at : at + block.shape[0], :] = block[:, c * lanes : (c + 1) * lanes]
            at += block.shape[0]
        message[at:, :] = pair


def up_kernel(peers, adapters, crossing, *refs):
    got = refs[:peers]
    rank_ref, slot_ref, up_ref = refs[peers : peers + 3]
    outs = refs[peers + 3 :]
    total = rank_ref[...]
    count, width = total.shape
    for ref in got:
        pair = ref[ref.shape[0] - count :, :].astype(f32)
        total = total + (pair[:, :width] + pair[:, width:])
    slots = slot_ref[:, :width]
    wide = jnp.concatenate(
        [jnp.where(slots == a + 1.0, total, 0.0) for a in range(adapters)], axis=1
    )
    upper = wide.astype(bf16)
    lower = (wide - upper.astype(f32)).astype(bf16)
    half = outs[0].shape[1]
    first = pl.multiple_of(lax.axis_index("tensor") // 2 * 2 * half, 2 * half)
    factor = up_ref[:, pl.ds(first, 2 * half)]
    term = jnp.dot(upper, factor, preferred_element_type=f32)
    term = adapter_scale * (term + jnp.dot(lower, factor, preferred_element_type=f32))
    term = term.astype(bf16).astype(f32)
    odd = lax.axis_index("tensor") % 2 == 1
    own = jnp.where(odd, term[:, half:], term[:, :half])
    if not crossing:
        outs[0][...] = own.astype(bf16)
        return
    other = jnp.where(odd, term[:, :half], term[:, half:])
    size = outs[0].shape[0]
    outs[0][...] = own[:size].astype(bf16)
    even_order, odd_order = orders(len(outs))
    for d in range(1, len(outs)):
        a, b = even_order.index(d) * size, odd_order.index(d) * size
        outs[d][...] = jnp.where(odd, other[b : b + size], other[a : a + size]).astype(bf16)


def sum_kernel(peers, blocks, capacity, relative, *refs):
    got = refs[:peers]
    base_ref, bias_ref, home_ref, out, place_ref = refs[peers:]
    place = placement(home_ref[...], blocks, capacity, relative, False)
    place_ref[...] = place.astype(f32).astype(bf16)
    total = base_ref[lax.axis_index("tensor")] + bias_ref[...]
    rows = total.shape[0]
    for c in range(total.shape[1] // lanes):
        part = total[:, c * lanes : (c + 1) * lanes]
        for ref in got:
            part = part + ref[c * rows : (c + 1) * rows, :].astype(f32)
        out[:, c * lanes : (c + 1) * lanes] = part


def last_kernel(pieces, *refs):
    got = refs[:pieces]
    place_ref, base_ref, cached_ref, fresh_ref, context_ref, values_ref = refs[pieces:]
    terms = jnp.concatenate([ref[...] for ref in got], axis=0)
    picked = jnp.dot(place_ref[...], terms, preferred_element_type=f32)
    values = (base_ref[...] + picked).astype(bf16)
    heads, size = values_ref.shape[1:]
    group = cached_ref.shape[1] // heads
    for h in range(heads):
        value = values[:, h * size : (h + 1) * size].astype(f32)
        values_ref[:, h, :] = value.astype(bf16)
        own = slice(h * group, (h + 1) * group)
        context = cached_ref[:, own, :] + fresh_ref[:, own, :] * value[:, None, :]
        context_ref[:, own, :] = context.astype(bf16)


def base_kernel(rows_ref, matrix_ref, out):
    parts, _, width = out.shape
    for t in range(parts):
        block = matrix_ref[:, t * width : (t + 1) * width]
        out[t] = jnp.dot(rows_ref[...], block, preferred_element_type=f32)


def base_product(rows, matrix, parts):
    count, depth = rows.shape
    width = matrix.shape[1] // parts
    return call(
        base_kernel,
        "base",
        [struct((parts, count, width), f32)],
        [rows, matrix],
        2 * count * depth * matrix.shape[1],
        in_specs=[VMEM] * 2,
        out_specs=[VMEM],
    )[0]


def attention_kernel(
    length_ref, query_ref, key_ref, value_ref, new_ref, cached_ref, fresh_ref, score_ref, prob_ref
):
    requests, heads, length, size = key_ref.shape
    group = query_ref.shape[1] // heads
    scale = 1.0 / size**0.5
    count = requests * heads
    across = (((1,), (1,)), ((), ()))
    pairs = [(r, h) for r in range(requests) for h in range(heads)]
    for i, (r, h) in enumerate(pairs):
        query = query_ref[r, h * group : (h + 1) * group, :]
        score_ref[i] = lax.dot_general(query, key_ref[r, h], across, preferred_element_type=f32)
    filled = jnp.concatenate(
        [jnp.full((heads, 1, length), length_ref[r], jnp.int32) for r in range(requests)], axis=0
    )
    valid = lax.broadcasted_iota(jnp.int32, (count, group, length), 2) < filled
    scores = jnp.where(valid, score_ref[...] * scale, -1e30)
    query = query_ref[...].reshape(count, group, size).astype(f32)
    new = new_ref[...].astype(f32).reshape(count, 1, size)
    fresh = jnp.sum(query * new, axis=2, keepdims=True) * scale
    top = jnp.maximum(jnp.max(scores, axis=2, keepdims=True), fresh)
    weights = jnp.exp(scores - top)
    alone = jnp.exp(fresh - top)
    total = jnp.sum(weights, axis=2, keepdims=True) + alone
    prob_ref[...] = (weights / total).astype(bf16)
    share = jnp.broadcast_to((alone / total).astype(bf16).astype(f32), (count, group, size))
    fresh_ref[...] = share.reshape(requests, heads * group, size)
    for i, (r, h) in enumerate(pairs):
        own = slice(h * group, (h + 1) * group)
        cached_ref[r, own, :] = jnp.dot(prob_ref[i], value_ref[r, h], preferred_element_type=f32)


def attention(lengths, queries, keys, values, new_keys):
    rows, heads, length, size = keys.shape
    query_heads = queries.shape[1]
    group = query_heads // heads
    shape = struct((rows, query_heads, size), f32)
    return call(
        attention_kernel,
        "attention",
        [shape, shape],
        [lengths, queries, keys, values, new_keys],
        4 * rows * query_heads * length * size,
        in_specs=[pl.BlockSpec(memory_space=pltpu.SMEM)] + [VMEM] * 4,
        out_specs=[VMEM] * 2,
        scratch_shapes=[
            pltpu.VMEM((rows * heads, group, length), f32),
            pltpu.VMEM((rows * heads, group, length), bf16),
        ],
    )


def send(block, target):
    replicas, parts = lax.axis_size("replica"), lax.axis_size("tensor")
    pairs = []
    for r in range(replicas):
        for t in range(parts):
            to_r, to_t = target(r, t)
            pairs.append((r * parts + t, to_r * parts + to_t))
    return lax.ppermute(block, ("replica", "tensor"), pairs)


def per_device(
    activations,
    value_matrix,
    value_offset_bias,
    adapter_down_factors,
    adapter_up_factors,
    adapter_replica,
    adapter_position,
    queries,
    cached_key_rows,
    cached_value_rows,
    incoming_keys,
    lengths,
):
    rows, features = activations.shape
    replicas = lax.axis_size("replica")
    parts = lax.axis_size("tensor")
    capacity = max(2, 2 * rows // replicas)
    adapters, rank, _ = adapter_down_factors.shape
    width = value_matrix.shape[1] // parts
    heads, size = incoming_keys.shape[1:]
    slots = replicas * capacity
    direct = capacity % 16 == 0
    home_row = adapter_replica.reshape(1, rows)

    def shuffle(block):
        block = block.reshape(replicas, capacity, -1)
        block = lax.all_to_all(block, "replica", split_axis=0, concat_axis=0, tiled=True)
        return block.reshape(slots, -1)

    pieces = replicas if direct else 1
    piece = slots // pieces
    local_rows, *packed = call(
        functools.partial(pack_kernel, replicas, capacity, direct),
        "pack",
        [struct(activations.shape, bf16)] + [struct((piece, features + lanes), bf16)] * pieces,
        [stay(home_row), stay(adapter_position.reshape(1, rows)), stay(activations)],
        pack_cost,
        in_specs=[HBM] * 3,
        out_specs=[VMEM] * (pieces + 1),
        scratch_shapes=[
            pltpu.VMEM((1, rows), jnp.int32),
            pltpu.VMEM((1, rows), jnp.int32),
            pltpu.SemaphoreType.DMA((3,)),
        ],
    )
    if direct:
        got = packed[:1]
        for block, a, b in list(zip(packed, *orders(replicas)))[1:]:
            got.append(send(block, lambda r, t: (r ^ (b if t % 2 else a), t)))
    else:
        got = [shuffle(packed[0])]
    base = base_product(local_rows, value_matrix, parts)
    cached, fresh = attention(
        lengths, queries, cached_key_rows, cached_value_rows, incoming_keys
    )
    base, cached, fresh = lax.optimization_barrier((base, cached, fresh))
    long = rows * (width // lanes) + slots
    rank_own, slot_ids, *messages = call(
        functools.partial(rank_kernel, pieces, adapters),
        "rank",
        [struct((slots, rank), f32), struct((slots, lanes), f32)]
        + [struct((long, lanes), bf16)] * (parts - 1),
        [*got, adapter_down_factors.reshape(adapters * rank, features), base],
        2 * slots * adapters * rank * features,
        in_specs=[VMEM] * (pieces + 2),
        out_specs=[VMEM] * (parts + 1),
    )
    heard = [send(m, lambda r, t: (r, t ^ (d + 1))) for d, m in enumerate(messages)]
    up_rows = adapter_up_factors.reshape(adapters * rank, parts * width)
    terms = call(
        functools.partial(up_kernel, parts - 1, adapters, direct),
        "up",
        [struct((piece, width), bf16)] * pieces,
        [*heard, rank_own, slot_ids, up_rows],
        8 * slots * adapters * rank * width,
        in_specs=[VMEM] * (parts + 2),
        out_specs=[VMEM] * pieces,
    )
    if direct:
        returned = [terms[0]]
        for d in range(1, replicas):
            returned.append(send(terms[d], lambda r, t: (r ^ d, t ^ 1)))
    else:
        returned = [shuffle(terms[0])]
    total, place = call(
        functools.partial(sum_kernel, parts - 1, replicas, capacity, direct),
        "base_sum",
        [struct((rows, width), f32), struct((rows, slots), bf16)],
        [*heard, base, value_offset_bias.reshape(1, width), home_row],
        parts * rows * width,
        in_specs=[VMEM] * (parts + 2),
        out_specs=[VMEM] * 2,
    )
    context, values = call(
        functools.partial(last_kernel, pieces),
        "last",
        [struct(queries.shape, bf16), struct((rows, heads, size), bf16)],
        [*returned, place, total, cached, fresh],
        2 * rows * slots * width,
        in_specs=[VMEM] * (pieces + 4),
        out_specs=[VMEM] * 2,
    )
    return (context, values)


def solution(mesh):
    rows = P(("groups", "replica"))
    split = P(("groups", "replica"), "tensor")
    in_specs = (
        split,
        P("tensor", None),
        P("tensor"),
        P(("groups", "replica"), None, "tensor"),
        rows,
        rows,
        rows,
        split,
        split,
        split,
        split,
        rows,
    )
    return jax.shard_map(
        per_device, mesh=mesh, in_specs=in_specs, out_specs=(split, split), check_vma=False
    )
```

```python
import functools

import jax
import jax.numpy as jnp
from jax import lax
from jax.experimental import pallas as pl
from jax.experimental.pallas import tpu as pltpu
from jax.sharding import PartitionSpec as P

adapter_scale = 0.5
pack_cost = 40_000_000_000
lanes = 128
f32 = jnp.float32
bf16 = jnp.bfloat16
VMEM = pl.BlockSpec(memory_space=pltpu.VMEM)
HBM = pl.BlockSpec(memory_space=pltpu.HBM)


def call(kernel, name, outs, args, flops, limit=16 << 20, **more):
    read = sum(a.size * a.dtype.itemsize for a in args)
    write = sum(o.size * o.dtype.itemsize for o in outs)
    return pl.pallas_call(
        kernel,
        name=name,
        out_shape=outs,
        cost_estimate=pl.CostEstimate(flops=flops, bytes_accessed=read + write, transcendentals=0),
        compiler_params=pltpu.CompilerParams(vmem_limit_bytes=limit),
        **more,
    )(*args)


def stay(array):
    return pltpu.with_memory_space_constraint(array, pltpu.HBM)


def struct(shape, dtype):
    return jax.ShapeDtypeStruct(shape, dtype)


def column(row):
    count = row.shape[1]
    square = lax.broadcasted_iota(jnp.int32, (count, count), 0) == lax.broadcasted_iota(
        jnp.int32, (count, count), 1
    )
    return jnp.sum(jnp.where(square, row, 0), axis=1, keepdims=True)


def orders(blocks):
    if blocks == 4:
        return [0, 2, 1, 3], [0, 2, 1, 3]
    return list(range(blocks)), list(range(blocks))


def tensor_order(parts):
    return [3, 2, 1] if parts == 4 else list(range(1, parts))


def return_order(pieces):
    return [3, 2, 1] if pieces == 4 else list(range(1, pieces))


def placement(home_row, blocks, capacity, relative, ordered):
    home = column(home_row)
    rows = home.shape[0]
    if relative:
        step = home ^ lax.axis_index("replica")
        home = step
        if ordered:
            odd = lax.axis_index("tensor") % 2 == 1
            for at, (a, b) in enumerate(zip(*orders(blocks))):
                home = jnp.where(step == jnp.where(odd, b, a), at, home)
    hot = (home == lax.broadcasted_iota(jnp.int32, (rows, blocks), 1)).astype(f32)
    at = lax.broadcasted_iota(jnp.int32, (rows, rows), 0)
    below = (lax.broadcasted_iota(jnp.int32, (rows, rows), 1) < at).astype(bf16)
    before = jnp.dot(below, hot.astype(bf16), preferred_element_type=f32)
    position = jnp.sum(before * hot, axis=1, keepdims=True).astype(jnp.int32)
    flat = home * capacity + position
    return flat == lax.broadcasted_iota(jnp.int32, (rows, blocks * capacity), 1)


def pack_kernel(blocks, capacity, relative, home_hbm, slot_hbm, rows_hbm, rows_ref, *refs):
    outs, (home_ref, slot_ref, semaphores) = refs[:-3], refs[-3:]
    copies = [
        pltpu.make_async_copy(source, target, semaphores.at[i])
        for i, (source, target) in enumerate(
            [(home_hbm, home_ref), (slot_hbm, slot_ref), (rows_hbm, rows_ref)]
        )
    ]
    for copy in copies:
        copy.start()
    copies[0].wait()
    place = placement(home_ref[...], blocks, capacity, relative, True)
    rows, width = rows_ref.shape
    copies[1].wait()
    slot = (column(slot_ref[...]) + 1).astype(f32)
    spread = jnp.broadcast_to(slot, (rows, lanes)).astype(bf16)
    turned = place.astype(f32).astype(bf16)
    over = (((0,), (0,)), ((), ()))
    slots = lax.dot_general(turned, spread, over, preferred_element_type=f32).astype(bf16)
    copies[2].wait()
    packed = lax.dot_general(turned, rows_ref[...], over, preferred_element_type=f32).astype(bf16)
    size = outs[0].shape[0]
    for b, out in enumerate(outs):
        out[:, :width] = packed[b * size : (b + 1) * size]
        out[:, width:] = slots[b * size : (b + 1) * size]


def rank_kernel(pieces, adapters, *refs):
    got = refs[:pieces]
    down_ref, base_ref, rank_ref, slot_ref = refs[pieces : pieces + 4]
    messages = refs[pieces + 4 :]
    features = down_ref.shape[1]
    rows = jnp.concatenate([ref[:, :features] for ref in got], axis=0)
    slots = jnp.concatenate([ref[:, features:] for ref in got], axis=0).astype(f32)
    slot_ref[...] = slots
    across = (((1,), (1,)), ((), ()))
    projected = lax.dot_general(rows, down_ref[...], across, preferred_element_type=f32)
    width = down_ref.shape[0] // adapters
    total = None
    for a in range(adapters):
        term = projected[:, a * width : (a + 1) * width]
        term = jnp.where(slots[:, :width] == a + 1.0, term, 0.0)
        total = term if total is None else total + term
    rank_ref[...] = total
    upper = total.astype(bf16)
    lower = (total - upper.astype(f32)).astype(bf16)
    pair = jnp.concatenate([upper, lower], axis=1)
    me = lax.axis_index("tensor")
    for d, message in enumerate(messages):
        block = base_ref[me ^ (d + 1)].astype(bf16)
        at = 0
        for c in range(block.shape[1] // lanes):
            message[at : at + block.shape[0], :] = block[:, c * lanes : (c + 1) * lanes]
            at += block.shape[0]
        message[at:, :] = pair


def up_kernel(peers, adapters, crossing, *refs):
    got = refs[:peers]
    rank_ref, slot_ref, up_ref = refs[peers : peers + 3]
    outs = refs[peers + 3 :]
    total = rank_ref[...]
    count, width = total.shape
    for ref in got:
        pair = ref[ref.shape[0] - count :, :].astype(f32)
        total = total + (pair[:, :width] + pair[:, width:])
    slots = slot_ref[:, :width]
    wide = jnp.concatenate(
        [jnp.where(slots == a + 1.0, total, 0.0) for a in range(adapters)], axis=1
    )
    upper = wide.astype(bf16)
    lower = (wide - upper.astype(f32)).astype(bf16)
    half = outs[0].shape[1]
    first = pl.multiple_of(lax.axis_index("tensor") // 2 * 2 * half, 2 * half)
    factor = up_ref[:, pl.ds(first, 2 * half)]
    term = jnp.dot(upper, factor, preferred_element_type=f32)
    term = adapter_scale * (term + jnp.dot(lower, factor, preferred_element_type=f32))
    term = term.astype(bf16).astype(f32)
    odd = lax.axis_index("tensor") % 2 == 1
    own = jnp.where(odd, term[:, half:], term[:, :half])
    if not crossing:
        outs[0][...] = own.astype(bf16)
        return
    other = jnp.where(odd, term[:, :half], term[:, half:])
    size = outs[0].shape[0]
    outs[0][...] = own[:size].astype(bf16)
    even_order, odd_order = orders(len(outs))
    for d in range(1, len(outs)):
        a, b = even_order.index(d) * size, odd_order.index(d) * size
        outs[d][...] = jnp.where(odd, other[b : b + size], other[a : a + size]).astype(bf16)


def sum_kernel(peers, blocks, capacity, relative, *refs):
    got = refs[:peers]
    base_ref, bias_ref, home_ref, out, place_ref = refs[peers:]
    place = placement(home_ref[...], blocks, capacity, relative, False)
    place_ref[...] = place.astype(f32).astype(bf16)
    total = base_ref[lax.axis_index("tensor")] + bias_ref[...]
    rows = total.shape[0]
    for c in range(total.shape[1] // lanes):
        part = total[:, c * lanes : (c + 1) * lanes]
        for ref in got:
            part = part + ref[c * rows : (c + 1) * rows, :].astype(f32)
        out[:, c * lanes : (c + 1) * lanes] = part


def last_kernel(pieces, *refs):
    got = refs[:pieces]
    place_ref, base_ref, cached_ref, fresh_ref, context_ref, values_ref = refs[pieces:]
    at = [0] + [1 + return_order(pieces).index(d) for d in range(1, pieces)]
    terms = jnp.concatenate([got[i][...] for i in at], axis=0)
    picked = jnp.dot(place_ref[...], terms, preferred_element_type=f32)
    values = (base_ref[...] + picked).astype(bf16)
    heads, size = values_ref.shape[1:]
    group = cached_ref.shape[1] // heads
    for h in range(heads):
        value = values[:, h * size : (h + 1) * size].astype(f32)
        values_ref[:, h, :] = value.astype(bf16)
        own = slice(h * group, (h + 1) * group)
        context = cached_ref[:, own, :] + fresh_ref[:, own, :] * value[:, None, :]
        context_ref[:, own, :] = context.astype(bf16)


def base_kernel(rows_ref, matrix_ref, out):
    parts, _, width = out.shape
    for t in range(parts):
        block = matrix_ref[:, t * width : (t + 1) * width]
        out[t] = jnp.dot(rows_ref[...], block, preferred_element_type=f32)


def base_product(rows, matrix, parts):
    count, depth = rows.shape
    width = matrix.shape[1] // parts
    return call(
        base_kernel,
        "base",
        [struct((parts, count, width), f32)],
        [rows, matrix],
        2 * count * depth * matrix.shape[1],
        in_specs=[VMEM] * 2,
        out_specs=[VMEM],
    )[0]


def attention_kernel(
    length_ref, query_ref, key_ref, value_ref, new_ref, cached_ref, fresh_ref, score_ref, prob_ref
):
    requests, heads, length, size = key_ref.shape
    group = query_ref.shape[1] // heads
    scale = 1.0 / size**0.5
    count = requests * heads
    across = (((1,), (1,)), ((), ()))
    pairs = [(r, h) for r in range(requests) for h in range(heads)]
    for i, (r, h) in enumerate(pairs):
        query = query_ref[r, h * group : (h + 1) * group, :]
        score_ref[i] = lax.dot_general(query, key_ref[r, h], across, preferred_element_type=f32)
    filled = jnp.concatenate(
        [jnp.full((heads, 1, length), length_ref[r], jnp.int32) for r in range(requests)], axis=0
    )
    valid = lax.broadcasted_iota(jnp.int32, (count, group, length), 2) < filled
    scores = jnp.where(valid, score_ref[...] * scale, -1e30)
    query = query_ref[...].reshape(count, group, size).astype(f32)
    new = new_ref[...].astype(f32).reshape(count, 1, size)
    fresh = jnp.sum(query * new, axis=2, keepdims=True) * scale
    top = jnp.maximum(jnp.max(scores, axis=2, keepdims=True), fresh)
    weights = jnp.exp(scores - top)
    alone = jnp.exp(fresh - top)
    total = jnp.sum(weights, axis=2, keepdims=True) + alone
    prob_ref[...] = (weights / total).astype(bf16)
    share = jnp.broadcast_to((alone / total).astype(bf16).astype(f32), (count, group, size))
    fresh_ref[...] = share.reshape(requests, heads * group, size)
    for i, (r, h) in enumerate(pairs):
        own = slice(h * group, (h + 1) * group)
        cached_ref[r, own, :] = jnp.dot(prob_ref[i], value_ref[r, h], preferred_element_type=f32)


def attention(lengths, queries, keys, values, new_keys):
    rows, heads, length, size = keys.shape
    query_heads = queries.shape[1]
    group = query_heads // heads
    shape = struct((rows, query_heads, size), f32)
    return call(
        attention_kernel,
        "attention",
        [shape, shape],
        [lengths, queries, keys, values, new_keys],
        4 * rows * query_heads * length * size,
        in_specs=[pl.BlockSpec(memory_space=pltpu.SMEM)] + [VMEM] * 4,
        out_specs=[VMEM] * 2,
        scratch_shapes=[
            pltpu.VMEM((rows * heads, group, length), f32),
            pltpu.VMEM((rows * heads, group, length), bf16),
        ],
    )


def send(block, target):
    replicas, parts = lax.axis_size("replica"), lax.axis_size("tensor")
    pairs = []
    for r in range(replicas):
        for t in range(parts):
            to_r, to_t = target(r, t)
            pairs.append((r * parts + t, to_r * parts + to_t))
    return lax.ppermute(block, ("replica", "tensor"), pairs)


def per_device(
    activations,
    value_matrix,
    value_offset_bias,
    adapter_down_factors,
    adapter_up_factors,
    adapter_replica,
    adapter_position,
    queries,
    cached_key_rows,
    cached_value_rows,
    incoming_keys,
    lengths,
):
    rows, features = activations.shape
    replicas = lax.axis_size("replica")
    parts = lax.axis_size("tensor")
    capacity = max(2, 2 * rows // replicas)
    adapters, rank, _ = adapter_down_factors.shape
    width = value_matrix.shape[1] // parts
    heads, size = incoming_keys.shape[1:]
    slots = replicas * capacity
    direct = capacity % 16 == 0
    home_row = adapter_replica.reshape(1, rows)

    def shuffle(block):
        block = block.reshape(replicas, capacity, -1)
        block = lax.all_to_all(block, "replica", split_axis=0, concat_axis=0, tiled=True)
        return block.reshape(slots, -1)

    pieces = replicas if direct else 1
    piece = slots // pieces
    local_rows, *packed = call(
        functools.partial(pack_kernel, replicas, capacity, direct),
        "pack",
        [struct(activations.shape, bf16)] + [struct((piece, features + lanes), bf16)] * pieces,
        [stay(home_row), stay(adapter_position.reshape(1, rows)), stay(activations)],
        pack_cost,
        in_specs=[HBM] * 3,
        out_specs=[VMEM] * (pieces + 1),
        scratch_shapes=[
            pltpu.VMEM((1, rows), jnp.int32),
            pltpu.VMEM((1, rows), jnp.int32),
            pltpu.SemaphoreType.DMA((3,)),
        ],
    )
    if direct:
        got = packed[:1]
        for block, a, b in list(zip(packed, *orders(replicas)))[1:]:
            got.append(send(block, lambda r, t: (r ^ (b if t % 2 else a), t)))
    else:
        got = [shuffle(packed[0])]
    base = base_product(local_rows, value_matrix, parts)
    cached, fresh = attention(
        lengths, queries, cached_key_rows, cached_value_rows, incoming_keys
    )
    base, cached, fresh = lax.optimization_barrier((base, cached, fresh))
    long = rows * (width // lanes) + slots
    rank_own, slot_ids, *messages = call(
        functools.partial(rank_kernel, pieces, adapters),
        "rank",
        [struct((slots, rank), f32), struct((slots, lanes), f32)]
        + [struct((long, lanes), bf16)] * (parts - 1),
        [*got, adapter_down_factors.reshape(adapters * rank, features), base],
        2 * slots * adapters * rank * features,
        in_specs=[VMEM] * (pieces + 2),
        out_specs=[VMEM] * (parts + 1),
    )
    heard = [send(messages[d - 1], lambda r, t: (r, t ^ d)) for d in tensor_order(parts)]
    up_rows = adapter_up_factors.reshape(adapters * rank, parts * width)
    terms = call(
        functools.partial(up_kernel, parts - 1, adapters, direct),
        "up",
        [struct((piece, width), bf16)] * pieces,
        [*heard, rank_own, slot_ids, up_rows],
        8 * slots * adapters * rank * width,
        in_specs=[VMEM] * (parts + 2),
        out_specs=[VMEM] * pieces,
    )
    if direct:
        returned = [terms[0]]
        for d in return_order(replicas):
            returned.append(send(terms[d], lambda r, t: (r ^ d, t ^ 1)))
    else:
        returned = [shuffle(terms[0])]
    total, place = call(
        functools.partial(sum_kernel, parts - 1, replicas, capacity, direct),
        "base_sum",
        [struct((rows, width), f32), struct((rows, slots), bf16)],
        [*heard, base, value_offset_bias.reshape(1, width), home_row],
        parts * rows * width,
        in_specs=[VMEM] * (parts + 2),
        out_specs=[VMEM] * 2,
    )
    context, values = call(
        functools.partial(last_kernel, pieces),
        "last",
        [struct(queries.shape, bf16), struct((rows, heads, size), bf16)],
        [*returned, place, total, cached, fresh],
        2 * rows * slots * width,
        in_specs=[VMEM] * (pieces + 4),
        out_specs=[VMEM] * 2,
    )
    return (context, values)


def solution(mesh):
    rows = P(("groups", "replica"))
    split = P(("groups", "replica"), "tensor")
    in_specs = (
        split,
        P("tensor", None),
        P("tensor"),
        P(("groups", "replica"), None, "tensor"),
        rows,
        rows,
        rows,
        split,
        split,
        split,
        split,
        rows,
    )
    return jax.shard_map(
        per_device, mesh=mesh, in_specs=in_specs, out_specs=(split, split), check_vma=False
    )
```

```python
import functools

import jax
import jax.numpy as jnp
from jax import lax
from jax.experimental import pallas as pl
from jax.experimental.pallas import tpu as pltpu
from jax.sharding import PartitionSpec as P

adapter_scale = 0.5
pack_cost = 40_000_000_000
lanes = 128
f32 = jnp.float32
bf16 = jnp.bfloat16
VMEM = pl.BlockSpec(memory_space=pltpu.VMEM)
HBM = pl.BlockSpec(memory_space=pltpu.HBM)


def call(kernel, name, outs, args, flops, limit=16 << 20, **more):
    read = sum(a.size * a.dtype.itemsize for a in args)
    write = sum(o.size * o.dtype.itemsize for o in outs)
    return pl.pallas_call(
        kernel,
        name=name,
        out_shape=outs,
        cost_estimate=pl.CostEstimate(flops=flops, bytes_accessed=read + write, transcendentals=0),
        compiler_params=pltpu.CompilerParams(vmem_limit_bytes=limit),
        **more,
    )(*args)


def stay(array):
    return pltpu.with_memory_space_constraint(array, pltpu.HBM)


def struct(shape, dtype):
    return jax.ShapeDtypeStruct(shape, dtype)


def column(row):
    count = row.shape[1]
    square = lax.broadcasted_iota(jnp.int32, (count, count), 0) == lax.broadcasted_iota(
        jnp.int32, (count, count), 1
    )
    return jnp.sum(jnp.where(square, row, 0), axis=1, keepdims=True)


def orders(blocks):
    if blocks == 4:
        return [0, 2, 1, 3], [0, 2, 1, 3]
    return list(range(blocks)), list(range(blocks))


def tensor_order(parts):
    return [3, 2, 1] if parts == 4 else list(range(1, parts))


def return_order(pieces):
    return [3, 2, 1] if pieces == 4 else list(range(1, pieces))


def labels(home, blocks, relative, ordered):
    if not relative:
        return home
    step = home ^ lax.axis_index("replica")
    if not ordered:
        return step
    odd = lax.axis_index("tensor") % 2 == 1
    for at, (a, b) in enumerate(zip(*orders(blocks))):
        home = jnp.where(step == jnp.where(odd, b, a), at, home)
    return home


def placement(home_row, blocks, capacity, relative):
    home = labels(column(home_row), blocks, relative, False)
    rows = home.shape[0]
    hot = (home == lax.broadcasted_iota(jnp.int32, (rows, blocks), 1)).astype(f32)
    at = lax.broadcasted_iota(jnp.int32, (rows, rows), 0)
    below = (lax.broadcasted_iota(jnp.int32, (rows, rows), 1) < at).astype(bf16)
    before = jnp.dot(below, hot.astype(bf16), preferred_element_type=f32)
    position = jnp.sum(before * hot, axis=1, keepdims=True).astype(jnp.int32)
    flat = home * capacity + position
    return flat == lax.broadcasted_iota(jnp.int32, (rows, blocks * capacity), 1)


def pack_kernel(blocks, capacity, relative, home_hbm, slot_hbm, rows_hbm, rows_ref, *refs):
    outs, (home_ref, slot_ref, semaphores) = refs[:-3], refs[-3:]
    copies = [
        pltpu.make_async_copy(source, target, semaphores.at[i])
        for i, (source, target) in enumerate(
            [(home_hbm, home_ref), (slot_hbm, slot_ref), (rows_hbm, rows_ref)]
        )
    ]
    for copy in copies:
        copy.start()
    rows, width = rows_ref.shape
    at = lax.broadcasted_iota(jnp.int32, (rows, rows), 0)
    above = (at < lax.broadcasted_iota(jnp.int32, (rows, rows), 1)).astype(f32).astype(bf16)
    copies[0].wait()
    label = labels(home_ref[...], blocks, relative, True)
    hot = (label == lax.broadcasted_iota(jnp.int32, (blocks, rows), 0)).astype(f32)
    before = jnp.dot(hot.astype(bf16), above, preferred_element_type=f32)
    position = jnp.sum(before * hot, axis=0, keepdims=True).astype(jnp.int32)
    flat = label * capacity + position
    turned = flat == lax.broadcasted_iota(jnp.int32, (blocks * capacity, rows), 0)
    copies[1].wait()
    slots = jnp.sum(jnp.where(turned, slot_ref[...] + 1, 0).astype(f32), axis=1, keepdims=True)
    slots = jnp.broadcast_to(slots, (blocks * capacity, lanes)).astype(bf16)
    turned = turned.astype(f32).astype(bf16)
    copies[2].wait()
    packed = jnp.dot(turned, rows_ref[...], preferred_element_type=f32).astype(bf16)
    size = outs[0].shape[0]
    for b, out in enumerate(outs):
        out[:, :width] = packed[b * size : (b + 1) * size]
        out[:, width:] = slots[b * size : (b + 1) * size]


def rank_kernel(pieces, adapters, *refs):
    got = refs[:pieces]
    down_ref, base_ref, rank_ref, slot_ref = refs[pieces : pieces + 4]
    messages = refs[pieces + 4 :]
    features = down_ref.shape[1]
    rows = jnp.concatenate([ref[:, :features] for ref in got], axis=0)
    slots = jnp.concatenate([ref[:, features:] for ref in got], axis=0).astype(f32)
    slot_ref[...] = slots
    across = (((1,), (1,)), ((), ()))
    projected = lax.dot_general(rows, down_ref[...], across, preferred_element_type=f32)
    width = down_ref.shape[0] // adapters
    total = None
    for a in range(adapters):
        term = projected[:, a * width : (a + 1) * width]
        term = jnp.where(slots[:, :width] == a + 1.0, term, 0.0)
        total = term if total is None else total + term
    rank_ref[...] = total
    upper = total.astype(bf16)
    lower = (total - upper.astype(f32)).astype(bf16)
    pair = jnp.concatenate([upper, lower], axis=1)
    me = lax.axis_index("tensor")
    for d, message in enumerate(messages):
        block = base_ref[me ^ (d + 1)].astype(bf16)
        at = 0
        for c in range(block.shape[1] // lanes):
            message[at : at + block.shape[0], :] = block[:, c * lanes : (c + 1) * lanes]
            at += block.shape[0]
        message[at:, :] = pair


def up_kernel(peers, adapters, crossing, *refs):
    got = refs[:peers]
    rank_ref, slot_ref, up_ref = refs[peers : peers + 3]
    outs = refs[peers + 3 :]
    total = rank_ref[...]
    count, width = total.shape
    for ref in got:
        pair = ref[ref.shape[0] - count :, :].astype(f32)
        total = total + (pair[:, :width] + pair[:, width:])
    slots = slot_ref[:, :width]
    wide = jnp.concatenate(
        [jnp.where(slots == a + 1.0, total, 0.0) for a in range(adapters)], axis=1
    )
    upper = wide.astype(bf16)
    lower = (wide - upper.astype(f32)).astype(bf16)
    half = outs[0].shape[1]
    first = pl.multiple_of(lax.axis_index("tensor") // 2 * 2 * half, 2 * half)
    factor = up_ref[:, pl.ds(first, 2 * half)]
    term = jnp.dot(upper, factor, preferred_element_type=f32)
    term = adapter_scale * (term + jnp.dot(lower, factor, preferred_element_type=f32))
    term = term.astype(bf16).astype(f32)
    odd = lax.axis_index("tensor") % 2 == 1
    own = jnp.where(odd, term[:, half:], term[:, :half])
    if not crossing:
        outs[0][...] = own.astype(bf16)
        return
    other = jnp.where(odd, term[:, :half], term[:, half:])
    size = outs[0].shape[0]
    outs[0][...] = own[:size].astype(bf16)
    even_order, odd_order = orders(len(outs))
    for d in range(1, len(outs)):
        a, b = even_order.index(d) * size, odd_order.index(d) * size
        outs[d][...] = jnp.where(odd, other[b : b + size], other[a : a + size]).astype(bf16)


def sum_kernel(peers, blocks, capacity, relative, *refs):
    got = refs[:peers]
    base_ref, bias_ref, home_ref, out, place_ref = refs[peers:]
    place = placement(home_ref[...], blocks, capacity, relative)
    place_ref[...] = place.astype(f32).astype(bf16)
    total = base_ref[lax.axis_index("tensor")] + bias_ref[...]
    rows = total.shape[0]
    for c in range(total.shape[1] // lanes):
        part = total[:, c * lanes : (c + 1) * lanes]
        for ref in got:
            part = part + ref[c * rows : (c + 1) * rows, :].astype(f32)
        out[:, c * lanes : (c + 1) * lanes] = part


def last_kernel(pieces, *refs):
    got = refs[:pieces]
    place_ref, base_ref, cached_ref, fresh_ref, context_ref, values_ref = refs[pieces:]
    at = [0] + [1 + return_order(pieces).index(d) for d in range(1, pieces)]
    terms = jnp.concatenate([got[i][...] for i in at], axis=0)
    picked = jnp.dot(place_ref[...], terms, preferred_element_type=f32)
    values = (base_ref[...] + picked).astype(bf16)
    heads, size = values_ref.shape[1:]
    group = cached_ref.shape[1] // heads
    for h in range(heads):
        value = values[:, h * size : (h + 1) * size].astype(f32)
        values_ref[:, h, :] = value.astype(bf16)
        own = slice(h * group, (h + 1) * group)
        context = cached_ref[:, own, :] + fresh_ref[:, own, :] * value[:, None, :]
        context_ref[:, own, :] = context.astype(bf16)


def base_kernel(rows_ref, matrix_ref, out):
    parts, _, width = out.shape
    for t in range(parts):
        block = matrix_ref[:, t * width : (t + 1) * width]
        out[t] = jnp.dot(rows_ref[...], block, preferred_element_type=f32)


def base_product(rows, matrix, parts):
    count, depth = rows.shape
    width = matrix.shape[1] // parts
    return call(
        base_kernel,
        "base",
        [struct((parts, count, width), f32)],
        [rows, matrix],
        2 * count * depth * matrix.shape[1],
        in_specs=[VMEM] * 2,
        out_specs=[VMEM],
    )[0]


def attention_kernel(
    length_ref, query_ref, key_ref, value_ref, new_ref, cached_ref, fresh_ref, score_ref, prob_ref
):
    requests, heads, length, size = key_ref.shape
    group = query_ref.shape[1] // heads
    scale = 1.0 / size**0.5
    count = requests * heads
    across = (((1,), (1,)), ((), ()))
    pairs = [(r, h) for r in range(requests) for h in range(heads)]
    for i, (r, h) in enumerate(pairs):
        query = query_ref[r, h * group : (h + 1) * group, :]
        score_ref[i] = lax.dot_general(query, key_ref[r, h], across, preferred_element_type=f32)
    filled = jnp.concatenate(
        [jnp.full((heads, 1, length), length_ref[r], jnp.int32) for r in range(requests)], axis=0
    )
    valid = lax.broadcasted_iota(jnp.int32, (count, group, length), 2) < filled
    scores = jnp.where(valid, score_ref[...] * scale, -1e30)
    query = query_ref[...].reshape(count, group, size).astype(f32)
    new = new_ref[...].astype(f32).reshape(count, 1, size)
    fresh = jnp.sum(query * new, axis=2, keepdims=True) * scale
    top = jnp.maximum(jnp.max(scores, axis=2, keepdims=True), fresh)
    weights = jnp.exp(scores - top)
    alone = jnp.exp(fresh - top)
    total = jnp.sum(weights, axis=2, keepdims=True) + alone
    prob_ref[...] = (weights / total).astype(bf16)
    share = jnp.broadcast_to((alone / total).astype(bf16).astype(f32), (count, group, size))
    fresh_ref[...] = share.reshape(requests, heads * group, size)
    for i, (r, h) in enumerate(pairs):
        own = slice(h * group, (h + 1) * group)
        cached_ref[r, own, :] = jnp.dot(prob_ref[i], value_ref[r, h], preferred_element_type=f32)


def attention(lengths, queries, keys, values, new_keys):
    rows, heads, length, size = keys.shape
    query_heads = queries.shape[1]
    group = query_heads // heads
    shape = struct((rows, query_heads, size), f32)
    return call(
        attention_kernel,
        "attention",
        [shape, shape],
        [lengths, queries, keys, values, new_keys],
        4 * rows * query_heads * length * size,
        in_specs=[pl.BlockSpec(memory_space=pltpu.SMEM)] + [VMEM] * 4,
        out_specs=[VMEM] * 2,
        scratch_shapes=[
            pltpu.VMEM((rows * heads, group, length), f32),
            pltpu.VMEM((rows * heads, group, length), bf16),
        ],
    )


def send(block, target):
    replicas, parts = lax.axis_size("replica"), lax.axis_size("tensor")
    pairs = []
    for r in range(replicas):
        for t in range(parts):
            to_r, to_t = target(r, t)
            pairs.append((r * parts + t, to_r * parts + to_t))
    return lax.ppermute(block, ("replica", "tensor"), pairs)


def per_device(
    activations,
    value_matrix,
    value_offset_bias,
    adapter_down_factors,
    adapter_up_factors,
    adapter_replica,
    adapter_position,
    queries,
    cached_key_rows,
    cached_value_rows,
    incoming_keys,
    lengths,
):
    rows, features = activations.shape
    replicas = lax.axis_size("replica")
    parts = lax.axis_size("tensor")
    capacity = max(2, 2 * rows // replicas)
    adapters, rank, _ = adapter_down_factors.shape
    width = value_matrix.shape[1] // parts
    heads, size = incoming_keys.shape[1:]
    slots = replicas * capacity
    direct = capacity % 16 == 0
    home_row = adapter_replica.reshape(1, rows)

    def shuffle(block):
        block = block.reshape(replicas, capacity, -1)
        block = lax.all_to_all(block, "replica", split_axis=0, concat_axis=0, tiled=True)
        return block.reshape(slots, -1)

    pieces = replicas if direct else 1
    piece = slots // pieces
    local_rows, *packed = call(
        functools.partial(pack_kernel, replicas, capacity, direct),
        "pack",
        [struct(activations.shape, bf16)] + [struct((piece, features + lanes), bf16)] * pieces,
        [stay(home_row), stay(adapter_position.reshape(1, rows)), stay(activations)],
        pack_cost,
        in_specs=[HBM] * 3,
        out_specs=[VMEM] * (pieces + 1),
        scratch_shapes=[
            pltpu.VMEM((1, rows), jnp.int32),
            pltpu.VMEM((1, rows), jnp.int32),
            pltpu.SemaphoreType.DMA((3,)),
        ],
    )
    if direct:
        got = packed[:1]
        for block, a, b in list(zip(packed, *orders(replicas)))[1:]:
            got.append(send(block, lambda r, t: (r ^ (b if t % 2 else a), t)))
    else:
        got = [shuffle(packed[0])]
    base = base_product(local_rows, value_matrix, parts)
    cached, fresh = attention(
        lengths, queries, cached_key_rows, cached_value_rows, incoming_keys
    )
    base, cached, fresh = lax.optimization_barrier((base, cached, fresh))
    long = rows * (width // lanes) + slots
    rank_own, slot_ids, *messages = call(
        functools.partial(rank_kernel, pieces, adapters),
        "rank",
        [struct((slots, rank), f32), struct((slots, lanes), f32)]
        + [struct((long, lanes), bf16)] * (parts - 1),
        [*got, adapter_down_factors.reshape(adapters * rank, features), base],
        2 * slots * adapters * rank * features,
        in_specs=[VMEM] * (pieces + 2),
        out_specs=[VMEM] * (parts + 1),
    )
    heard = [send(messages[d - 1], lambda r, t: (r, t ^ d)) for d in tensor_order(parts)]
    up_rows = adapter_up_factors.reshape(adapters * rank, parts * width)
    terms = call(
        functools.partial(up_kernel, parts - 1, adapters, direct),
        "up",
        [struct((piece, width), bf16)] * pieces,
        [*heard, rank_own, slot_ids, up_rows],
        8 * slots * adapters * rank * width,
        in_specs=[VMEM] * (parts + 2),
        out_specs=[VMEM] * pieces,
    )
    if direct:
        returned = [terms[0]]
        for d in return_order(replicas):
            returned.append(send(terms[d], lambda r, t: (r ^ d, t ^ 1)))
    else:
        returned = [shuffle(terms[0])]
    total, place = call(
        functools.partial(sum_kernel, parts - 1, replicas, capacity, direct),
        "base_sum",
        [struct((rows, width), f32), struct((rows, slots), bf16)],
        [*heard, base, value_offset_bias.reshape(1, width), home_row],
        parts * rows * width,
        in_specs=[VMEM] * (parts + 2),
        out_specs=[VMEM] * 2,
    )
    context, values = call(
        functools.partial(last_kernel, pieces),
        "last",
        [struct(queries.shape, bf16), struct((rows, heads, size), bf16)],
        [*returned, place, total, cached, fresh],
        2 * rows * slots * width,
        in_specs=[VMEM] * (pieces + 4),
        out_specs=[VMEM] * 2,
    )
    return (context, values)


def solution(mesh):
    rows = P(("groups", "replica"))
    split = P(("groups", "replica"), "tensor")
    in_specs = (
        split,
        P("tensor", None),
        P("tensor"),
        P(("groups", "replica"), None, "tensor"),
        rows,
        rows,
        rows,
        split,
        split,
        split,
        split,
        rows,
    )
    return jax.shard_map(
        per_device, mesh=mesh, in_specs=in_specs, out_specs=(split, split), check_vma=False
    )
```

```python
import functools

import jax
import jax.numpy as jnp
from jax import lax
from jax.experimental import pallas as pl
from jax.experimental.pallas import tpu as pltpu
from jax.sharding import PartitionSpec as P

adapter_scale = 0.5
pack_cost = 40_000_000_000
lanes = 128
f32 = jnp.float32
bf16 = jnp.bfloat16
VMEM = pl.BlockSpec(memory_space=pltpu.VMEM)
HBM = pl.BlockSpec(memory_space=pltpu.HBM)


def call(kernel, name, outs, args, flops, limit=16 << 20, **more):
    read = sum(a.size * a.dtype.itemsize for a in args)
    write = sum(o.size * o.dtype.itemsize for o in outs)
    return pl.pallas_call(
        kernel,
        name=name,
        out_shape=outs,
        cost_estimate=pl.CostEstimate(flops=flops, bytes_accessed=read + write, transcendentals=0),
        compiler_params=pltpu.CompilerParams(vmem_limit_bytes=limit),
        **more,
    )(*args)


def stay(array):
    return pltpu.with_memory_space_constraint(array, pltpu.HBM)


def struct(shape, dtype):
    return jax.ShapeDtypeStruct(shape, dtype)


def column(row):
    count = row.shape[1]
    square = lax.broadcasted_iota(jnp.int32, (count, count), 0) == lax.broadcasted_iota(
        jnp.int32, (count, count), 1
    )
    return jnp.sum(jnp.where(square, row, 0), axis=1, keepdims=True)


def orders(blocks):
    if blocks == 4:
        return [0, 2, 1, 3], [0, 2, 1, 3]
    return list(range(blocks)), list(range(blocks))


def tensor_order(parts):
    return [3, 2, 1] if parts == 4 else list(range(1, parts))


def return_order(pieces):
    return [3, 2, 1] if pieces == 4 else list(range(1, pieces))


def labels(home, blocks, relative, ordered):
    if not relative:
        return home
    step = home ^ lax.axis_index("replica")
    if not ordered:
        return step
    odd = lax.axis_index("tensor") % 2 == 1
    for at, (a, b) in enumerate(zip(*orders(blocks))):
        home = jnp.where(step == jnp.where(odd, b, a), at, home)
    return home


def placement(home_row, blocks, capacity, relative):
    home = labels(column(home_row), blocks, relative, False)
    rows = home.shape[0]
    hot = (home == lax.broadcasted_iota(jnp.int32, (rows, blocks), 1)).astype(f32)
    at = lax.broadcasted_iota(jnp.int32, (rows, rows), 0)
    below = (lax.broadcasted_iota(jnp.int32, (rows, rows), 1) < at).astype(bf16)
    before = jnp.dot(below, hot.astype(bf16), preferred_element_type=f32)
    position = jnp.sum(before * hot, axis=1, keepdims=True).astype(jnp.int32)
    flat = home * capacity + position
    return flat == lax.broadcasted_iota(jnp.int32, (rows, blocks * capacity), 1)


def pack_kernel(blocks, capacity, relative, home_hbm, slot_hbm, rows_hbm, rows_ref, *refs):
    outs, (home_ref, slot_ref, semaphores) = refs[:-3], refs[-3:]
    copies = [
        pltpu.make_async_copy(source, target, semaphores.at[i])
        for i, (source, target) in enumerate(
            [(home_hbm, home_ref), (slot_hbm, slot_ref), (rows_hbm, rows_ref)]
        )
    ]
    for copy in copies:
        copy.start()
    rows, width = rows_ref.shape
    at = lax.broadcasted_iota(jnp.int32, (rows, rows), 0)
    above = (at < lax.broadcasted_iota(jnp.int32, (rows, rows), 1)).astype(f32).astype(bf16)
    copies[0].wait()
    label = labels(home_ref[...], blocks, relative, True)
    hot = (label == lax.broadcasted_iota(jnp.int32, (blocks, rows), 0)).astype(f32)
    before = jnp.dot(hot.astype(bf16), above, preferred_element_type=f32)
    position = jnp.sum(before * hot, axis=0, keepdims=True).astype(jnp.int32)
    flat = label * capacity + position
    turned = flat == lax.broadcasted_iota(jnp.int32, (blocks * capacity, rows), 0)
    copies[1].wait()
    slots = jnp.sum(jnp.where(turned, slot_ref[...] + 1, 0).astype(f32), axis=1, keepdims=True)
    slots = jnp.broadcast_to(slots, (blocks * capacity, lanes)).astype(bf16)
    turned = turned.astype(f32).astype(bf16)
    copies[2].wait()
    packed = jnp.dot(turned, rows_ref[...], preferred_element_type=f32).astype(bf16)
    size = blocks * capacity // len(outs)
    for b, out in enumerate(outs):
        block, marks = packed[b * size : (b + 1) * size], slots[b * size : (b + 1) * size]
        if not relative:
            out[:, :width] = block
            out[:, width:] = marks
            continue
        for c in range(width // lanes):
            out[c * size : (c + 1) * size, :] = block[:, c * lanes : (c + 1) * lanes]
        half, wide = size // 2, lanes // 2
        out[size * (width // lanes) :, :] = jnp.concatenate(
            [marks[:half, :wide], marks[half:, :wide]], axis=1
        )


def rank_kernel(pieces, adapters, *refs):
    got = refs[:pieces]
    down_ref, base_ref, rank_ref, slot_ref = refs[pieces : pieces + 4]
    messages = refs[pieces + 4 :]
    features = down_ref.shape[0]
    if pieces == 1:
        rows, slots = got[0][:, :features], got[0][:, features:].astype(f32)
    else:
        size, tiles, wide = slot_ref.shape[0] // pieces, features // lanes, lanes // 2
        rows = jnp.concatenate(
            [
                jnp.concatenate([ref[c * size : (c + 1) * size, :] for ref in got], axis=0)
                for c in range(tiles)
            ],
            axis=1,
        )
        marks = [ref[tiles * size :, :].astype(f32) for ref in got]
        slots = jnp.concatenate([m[:, h : h + wide] for m in marks for h in (0, wide)], axis=0)
    slot_ref[...] = slots[:, : slot_ref.shape[1]]
    projected = jnp.dot(rows, down_ref[...], preferred_element_type=f32)
    width = down_ref.shape[1] // adapters
    total = None
    for a in range(adapters):
        term = projected[:, a * width : (a + 1) * width]
        term = jnp.where(slots[:, :width] == a + 1.0, term, 0.0)
        total = term if total is None else total + term
    rank_ref[...] = total
    upper = total.astype(bf16)
    lower = (total - upper.astype(f32)).astype(bf16)
    pair = jnp.concatenate([upper, lower], axis=1)
    me = lax.axis_index("tensor")
    for d, message in enumerate(messages):
        block = base_ref[me ^ (d + 1)].astype(bf16)
        at = 0
        for c in range(block.shape[1] // lanes):
            message[at : at + block.shape[0], :] = block[:, c * lanes : (c + 1) * lanes]
            at += block.shape[0]
        message[at:, :] = pair


def up_kernel(peers, adapters, crossing, *refs):
    got = refs[:peers]
    rank_ref, slot_ref, up_ref = refs[peers : peers + 3]
    outs = refs[peers + 3 :]
    total = rank_ref[...]
    count, width = total.shape
    for ref in got:
        pair = ref[ref.shape[0] - count :, :].astype(f32)
        total = total + (pair[:, :width] + pair[:, width:])
    slots = slot_ref[:, :width]
    wide = jnp.concatenate(
        [jnp.where(slots == a + 1.0, total, 0.0) for a in range(adapters)], axis=1
    )
    upper = wide.astype(bf16)
    lower = (wide - upper.astype(f32)).astype(bf16)
    half = outs[0].shape[1]
    first = pl.multiple_of(lax.axis_index("tensor") // 2 * 2 * half, 2 * half)
    factor = up_ref[:, pl.ds(first, 2 * half)]
    both = jnp.concatenate([upper, lower], axis=0)
    both = jnp.dot(both, factor, preferred_element_type=f32)
    term = adapter_scale * (both[:count] + both[count:])
    term = term.astype(bf16).astype(f32)
    odd = lax.axis_index("tensor") % 2 == 1
    own = jnp.where(odd, term[:, half:], term[:, :half])
    if not crossing:
        outs[0][...] = own.astype(bf16)
        return
    other = jnp.where(odd, term[:, :half], term[:, half:])
    size = outs[0].shape[0]
    outs[0][...] = own[:size].astype(bf16)
    even_order, odd_order = orders(len(outs))
    for d in range(1, len(outs)):
        a, b = even_order.index(d) * size, odd_order.index(d) * size
        outs[d][...] = jnp.where(odd, other[b : b + size], other[a : a + size]).astype(bf16)


def sum_kernel(peers, blocks, capacity, relative, *refs):
    got = refs[:peers]
    base_ref, bias_ref, home_ref, out, place_ref = refs[peers:]
    place = placement(home_ref[...], blocks, capacity, relative)
    place_ref[...] = place.astype(f32).astype(bf16)
    total = base_ref[lax.axis_index("tensor")] + bias_ref[...]
    rows = total.shape[0]
    for c in range(total.shape[1] // lanes):
        part = total[:, c * lanes : (c + 1) * lanes]
        for ref in got:
            part = part + ref[c * rows : (c + 1) * rows, :].astype(f32)
        out[:, c * lanes : (c + 1) * lanes] = part


def last_kernel(pieces, *refs):
    got = refs[:pieces]
    place_ref, base_ref, cached_ref, fresh_ref, context_ref, values_ref = refs[pieces:]
    at = [0] + [1 + return_order(pieces).index(d) for d in range(1, pieces)]
    terms = jnp.concatenate([got[i][...] for i in at], axis=0)
    picked = jnp.dot(place_ref[...], terms, preferred_element_type=f32)
    values = (base_ref[...] + picked).astype(bf16)
    heads, size = values_ref.shape[1:]
    group = cached_ref.shape[1] // heads
    for h in range(heads):
        value = values[:, h * size : (h + 1) * size].astype(f32)
        values_ref[:, h, :] = value.astype(bf16)
        own = slice(h * group, (h + 1) * group)
        context = cached_ref[:, own, :] + fresh_ref[:, own, :] * value[:, None, :]
        context_ref[:, own, :] = context.astype(bf16)


def turn_kernel(in_ref, out):
    out[...] = in_ref[...].T


def base_kernel(rows_ref, matrix_ref, out):
    parts, _, width = out.shape
    for t in range(parts):
        block = matrix_ref[:, t * width : (t + 1) * width]
        out[t] = jnp.dot(rows_ref[...], block, preferred_element_type=f32)


def base_product(rows, matrix, parts):
    count, depth = rows.shape
    width = matrix.shape[1] // parts
    return call(
        base_kernel,
        "base",
        [struct((parts, count, width), f32)],
        [rows, matrix],
        2 * count * depth * matrix.shape[1],
        in_specs=[VMEM] * 2,
        out_specs=[VMEM],
    )[0]


def attention_kernel(
    length_ref, query_ref, key_ref, value_ref, new_ref, cached_ref, fresh_ref, score_ref, prob_ref
):
    requests, heads, length, size = key_ref.shape
    group = query_ref.shape[1] // heads
    scale = 1.0 / size**0.5
    count = requests * heads
    across = (((1,), (1,)), ((), ()))
    pairs = [(r, h) for r in range(requests) for h in range(heads)]
    for i, (r, h) in enumerate(pairs):
        query = query_ref[r, h * group : (h + 1) * group, :]
        score_ref[i] = lax.dot_general(query, key_ref[r, h], across, preferred_element_type=f32)
    filled = jnp.concatenate(
        [jnp.full((heads, 1, length), length_ref[r], jnp.int32) for r in range(requests)], axis=0
    )
    valid = lax.broadcasted_iota(jnp.int32, (count, group, length), 2) < filled
    scores = jnp.where(valid, score_ref[...] * scale, -1e30)
    query = query_ref[...].reshape(count, group, size).astype(f32)
    new = new_ref[...].astype(f32).reshape(count, 1, size)
    fresh = jnp.sum(query * new, axis=2, keepdims=True) * scale
    top = jnp.maximum(jnp.max(scores, axis=2, keepdims=True), fresh)
    weights = jnp.exp(scores - top)
    alone = jnp.exp(fresh - top)
    total = jnp.sum(weights, axis=2, keepdims=True) + alone
    prob_ref[...] = (weights / total).astype(bf16)
    share = jnp.broadcast_to((alone / total).astype(bf16).astype(f32), (count, group, size))
    fresh_ref[...] = share.reshape(requests, heads * group, size)
    for i, (r, h) in enumerate(pairs):
        own = slice(h * group, (h + 1) * group)
        cached_ref[r, own, :] = jnp.dot(prob_ref[i], value_ref[r, h], preferred_element_type=f32)


def attention(lengths, queries, keys, values, new_keys):
    rows, heads, length, size = keys.shape
    query_heads = queries.shape[1]
    group = query_heads // heads
    shape = struct((rows, query_heads, size), f32)
    return call(
        attention_kernel,
        "attention",
        [shape, shape],
        [lengths, queries, keys, values, new_keys],
        4 * rows * query_heads * length * size,
        in_specs=[pl.BlockSpec(memory_space=pltpu.SMEM)] + [VMEM] * 4,
        out_specs=[VMEM] * 2,
        scratch_shapes=[
            pltpu.VMEM((rows * heads, group, length), f32),
            pltpu.VMEM((rows * heads, group, length), bf16),
        ],
    )


def send(block, target):
    replicas, parts = lax.axis_size("replica"), lax.axis_size("tensor")
    pairs = []
    for r in range(replicas):
        for t in range(parts):
            to_r, to_t = target(r, t)
            pairs.append((r * parts + t, to_r * parts + to_t))
    return lax.ppermute(block, ("replica", "tensor"), pairs)


def per_device(
    activations,
    value_matrix,
    value_offset_bias,
    adapter_down_factors,
    adapter_up_factors,
    adapter_replica,
    adapter_position,
    queries,
    cached_key_rows,
    cached_value_rows,
    incoming_keys,
    lengths,
):
    rows, features = activations.shape
    replicas = lax.axis_size("replica")
    parts = lax.axis_size("tensor")
    capacity = max(2, 2 * rows // replicas)
    adapters, rank, _ = adapter_down_factors.shape
    width = value_matrix.shape[1] // parts
    heads, size = incoming_keys.shape[1:]
    slots = replicas * capacity
    direct = capacity % 16 == 0
    home_row = adapter_replica.reshape(1, rows)

    def shuffle(block):
        block = block.reshape(replicas, capacity, -1)
        block = lax.all_to_all(block, "replica", split_axis=0, concat_axis=0, tiled=True)
        return block.reshape(slots, -1)

    pieces = replicas if direct else 1
    piece = slots // pieces
    message = (piece, features + lanes)
    if direct:
        message = (piece * (features // lanes) + piece // 2, lanes)
    local_rows, *packed = call(
        functools.partial(pack_kernel, replicas, capacity, direct),
        "pack",
        [struct(activations.shape, bf16)] + [struct(message, bf16)] * pieces,
        [stay(home_row), stay(adapter_position.reshape(1, rows)), stay(activations)],
        pack_cost,
        in_specs=[HBM] * 3,
        out_specs=[VMEM] * (pieces + 1),
        scratch_shapes=[
            pltpu.VMEM((1, rows), jnp.int32),
            pltpu.VMEM((1, rows), jnp.int32),
            pltpu.SemaphoreType.DMA((3,)),
        ],
    )
    if direct:
        got = packed[:1]
        for block, a, b in list(zip(packed, *orders(replicas)))[1:]:
            got.append(send(block, lambda r, t: (r ^ (b if t % 2 else a), t)))
    else:
        got = [shuffle(packed[0])]
    base = base_product(local_rows, value_matrix, parts)
    (down,) = call(
        turn_kernel,
        "turn",
        [struct((features, adapters * rank), bf16)],
        [adapter_down_factors.reshape(adapters * rank, features)],
        200_000_000,
        in_specs=[VMEM],
        out_specs=[VMEM],
    )
    long = rows * (width // lanes) + slots
    rank_own, slot_ids, *messages = call(
        functools.partial(rank_kernel, pieces, adapters),
        "rank",
        [struct((slots, rank), f32), struct((slots, rank), f32)]
        + [struct((long, lanes), bf16)] * (parts - 1),
        [*got, down, base],
        2 * slots * adapters * rank * features,
        in_specs=[VMEM] * (pieces + 2),
        out_specs=[VMEM] * (parts + 1),
    )
    heard = [send(messages[d - 1], lambda r, t: (r, t ^ d)) for d in tensor_order(parts)]
    rank_own, held_lengths = lax.optimization_barrier((rank_own, lengths))
    cached, fresh = attention(
        held_lengths, queries, cached_key_rows, cached_value_rows, incoming_keys
    )
    rank_own, cached, fresh = lax.optimization_barrier((rank_own, cached, fresh))
    up_rows = adapter_up_factors.reshape(adapters * rank, parts * width)
    terms = call(
        functools.partial(up_kernel, parts - 1, adapters, direct),
        "up",
        [struct((piece, width), bf16)] * pieces,
        [*heard, rank_own, slot_ids, up_rows],
        8 * slots * adapters * rank * width,
        in_specs=[VMEM] * (parts + 2),
        out_specs=[VMEM] * pieces,
    )
    if direct:
        returned = [terms[0]]
        for d in return_order(replicas):
            returned.append(send(terms[d], lambda r, t: (r ^ d, t ^ 1)))
    else:
        returned = [shuffle(terms[0])]
    total, place = call(
        functools.partial(sum_kernel, parts - 1, replicas, capacity, direct),
        "base_sum",
        [struct((rows, width), f32), struct((rows, slots), bf16)],
        [*heard, base, value_offset_bias.reshape(1, width), home_row],
        parts * rows * width,
        in_specs=[VMEM] * (parts + 2),
        out_specs=[VMEM] * 2,
    )
    context, values = call(
        functools.partial(last_kernel, pieces),
        "last",
        [struct(queries.shape, bf16), struct((rows, heads, size), bf16)],
        [*returned, place, total, cached, fresh],
        2 * rows * slots * width,
        in_specs=[VMEM] * (pieces + 4),
        out_specs=[VMEM] * 2,
    )
    return (context, values)


def solution(mesh):
    rows = P(("groups", "replica"))
    split = P(("groups", "replica"), "tensor")
    in_specs = (
        split,
        P("tensor", None),
        P("tensor"),
        P(("groups", "replica"), None, "tensor"),
        rows,
        rows,
        rows,
        split,
        split,
        split,
        split,
        rows,
    )
    return jax.shard_map(
        per_device, mesh=mesh, in_specs=in_specs, out_specs=(split, split), check_vma=False
    )
```

```python
import functools

import jax
import jax.numpy as jnp
from jax import lax
from jax.experimental import pallas as pl
from jax.experimental.pallas import tpu as pltpu
from jax.sharding import PartitionSpec as P

adapter_scale = 0.5
pack_cost = 40_000_000_000
lanes = 128
f32 = jnp.float32
bf16 = jnp.bfloat16
VMEM = pl.BlockSpec(memory_space=pltpu.VMEM)
HBM = pl.BlockSpec(memory_space=pltpu.HBM)


def call(kernel, name, outs, args, flops, limit=16 << 20, **more):
    read = sum(a.size * a.dtype.itemsize for a in args)
    write = sum(o.size * o.dtype.itemsize for o in outs)
    return pl.pallas_call(
        kernel,
        name=name,
        out_shape=outs,
        cost_estimate=pl.CostEstimate(flops=flops, bytes_accessed=read + write, transcendentals=0),
        compiler_params=pltpu.CompilerParams(vmem_limit_bytes=limit),
        **more,
    )(*args)


def stay(array):
    return pltpu.with_memory_space_constraint(array, pltpu.HBM)


def struct(shape, dtype):
    return jax.ShapeDtypeStruct(shape, dtype)


def column(row):
    count = row.shape[1]
    square = lax.broadcasted_iota(jnp.int32, (count, count), 0) == lax.broadcasted_iota(
        jnp.int32, (count, count), 1
    )
    return jnp.sum(jnp.where(square, row, 0), axis=1, keepdims=True)


def orders(blocks):
    if blocks == 4:
        return [0, 2, 1, 3], [0, 2, 1, 3]
    return list(range(blocks)), list(range(blocks))


def tensor_order(parts):
    return [3, 2, 1] if parts == 4 else list(range(1, parts))


def return_order(pieces):
    return [3, 2, 1] if pieces == 4 else list(range(1, pieces))


def labels(home, blocks, relative, ordered):
    if not relative:
        return home
    step = home ^ lax.axis_index("replica")
    if not ordered:
        return step
    odd = lax.axis_index("tensor") % 2 == 1
    for at, (a, b) in enumerate(zip(*orders(blocks))):
        home = jnp.where(step == jnp.where(odd, b, a), at, home)
    return home


def placement(home_row, blocks, capacity, relative):
    home = labels(column(home_row), blocks, relative, False)
    rows = home.shape[0]
    hot = (home == lax.broadcasted_iota(jnp.int32, (rows, blocks), 1)).astype(f32)
    at = lax.broadcasted_iota(jnp.int32, (rows, rows), 0)
    below = (lax.broadcasted_iota(jnp.int32, (rows, rows), 1) < at).astype(bf16)
    before = jnp.dot(below, hot.astype(bf16), preferred_element_type=f32)
    position = jnp.sum(before * hot, axis=1, keepdims=True).astype(jnp.int32)
    flat = home * capacity + position
    return flat == lax.broadcasted_iota(jnp.int32, (rows, blocks * capacity), 1)


def pack_kernel(blocks, capacity, relative, home_hbm, slot_hbm, rows_hbm, rows_ref, *refs):
    outs, (home_ref, slot_ref, semaphores) = refs[:-3], refs[-3:]
    copies = [
        pltpu.make_async_copy(source, target, semaphores.at[i])
        for i, (source, target) in enumerate(
            [(home_hbm, home_ref), (slot_hbm, slot_ref), (rows_hbm, rows_ref)]
        )
    ]
    for copy in copies:
        copy.start()
    rows, width = rows_ref.shape
    at = lax.broadcasted_iota(jnp.int32, (rows, rows), 0)
    above = (at < lax.broadcasted_iota(jnp.int32, (rows, rows), 1)).astype(f32).astype(bf16)
    copies[0].wait()
    label = labels(home_ref[...], blocks, relative, True)
    hot = (label == lax.broadcasted_iota(jnp.int32, (blocks, rows), 0)).astype(f32)
    before = jnp.dot(hot.astype(bf16), above, preferred_element_type=f32)
    position = jnp.sum(before * hot, axis=0, keepdims=True).astype(jnp.int32)
    flat = label * capacity + position
    turned = flat == lax.broadcasted_iota(jnp.int32, (blocks * capacity, rows), 0)
    copies[1].wait()
    slots = jnp.sum(jnp.where(turned, slot_ref[...] + 1, 0).astype(f32), axis=1, keepdims=True)
    slots = jnp.broadcast_to(slots, (blocks * capacity, lanes)).astype(bf16)
    turned = turned.astype(f32).astype(bf16)
    copies[2].wait()
    packed = jnp.dot(turned, rows_ref[...], preferred_element_type=f32).astype(bf16)
    size = blocks * capacity // len(outs)
    for b, out in enumerate(outs):
        block, marks = packed[b * size : (b + 1) * size], slots[b * size : (b + 1) * size]
        if not relative:
            out[:, :width] = block
            out[:, width:] = marks
            continue
        for c in range(width // lanes):
            out[c * size : (c + 1) * size, :] = block[:, c * lanes : (c + 1) * lanes]
        half, wide = size // 2, lanes // 2
        out[size * (width // lanes) :, :] = jnp.concatenate(
            [marks[:half, :wide], marks[half:, :wide]], axis=1
        )


def rank_kernel(pieces, adapters, *refs):
    got = refs[:pieces]
    down_ref, base_ref, rank_ref, slot_ref = refs[pieces : pieces + 4]
    messages = refs[pieces + 4 :]
    features = down_ref.shape[0]
    if pieces == 1:
        rows, slots = got[0][:, :features], got[0][:, features:].astype(f32)
    else:
        size, tiles, wide = slot_ref.shape[0] // pieces, features // lanes, lanes // 2
        rows = jnp.concatenate(
            [
                jnp.concatenate([ref[c * size : (c + 1) * size, :] for ref in got], axis=0)
                for c in range(tiles)
            ],
            axis=1,
        )
        marks = [ref[tiles * size :, :].astype(f32) for ref in got]
        slots = jnp.concatenate([m[:, h : h + wide] for m in marks for h in (0, wide)], axis=0)
    slot_ref[...] = slots[:, : slot_ref.shape[1]]
    projected = jnp.dot(rows, down_ref[...], preferred_element_type=f32)
    width = down_ref.shape[1] // adapters
    total = None
    for a in range(adapters):
        term = projected[:, a * width : (a + 1) * width]
        term = jnp.where(slots[:, :width] == a + 1.0, term, 0.0)
        total = term if total is None else total + term
    rank_ref[...] = total
    half = total.shape[0] // 2
    pair = jnp.concatenate([total[:half], total[half:]], axis=1).astype(bf16)
    me = lax.axis_index("tensor")
    for d, message in enumerate(messages):
        block = base_ref[me ^ (d + 1)].astype(bf16)
        at = 0
        for c in range(block.shape[1] // lanes):
            message[at : at + block.shape[0], :] = block[:, c * lanes : (c + 1) * lanes]
            at += block.shape[0]
        message[at:, :] = pair


def up_kernel(peers, adapters, crossing, *refs):
    got = refs[:peers]
    rank_ref, slot_ref, up_ref = refs[peers : peers + 3]
    outs = refs[peers + 3 :]
    total = rank_ref[...]
    count, width = total.shape
    for ref in got:
        pair = ref[ref.shape[0] - count // 2 :, :].astype(f32)
        total = total + jnp.concatenate([pair[:, :width], pair[:, width:]], axis=0)
    slots = slot_ref[:, :width]
    wide = jnp.concatenate(
        [jnp.where(slots == a + 1.0, total, 0.0) for a in range(adapters)], axis=1
    )
    upper = wide.astype(bf16)
    lower = (wide - upper.astype(f32)).astype(bf16)
    half = outs[0].shape[1]
    first = pl.multiple_of(lax.axis_index("tensor") // 2 * 2 * half, 2 * half)
    factor = up_ref[:, pl.ds(first, 2 * half)]
    both = jnp.concatenate([upper, lower], axis=0)
    both = jnp.dot(both, factor, preferred_element_type=f32)
    term = adapter_scale * (both[:count] + both[count:])
    term = term.astype(bf16).astype(f32)
    odd = lax.axis_index("tensor") % 2 == 1
    own = jnp.where(odd, term[:, half:], term[:, :half])
    if not crossing:
        outs[0][...] = own.astype(bf16)
        return
    other = jnp.where(odd, term[:, :half], term[:, half:])
    size = outs[0].shape[0]
    outs[0][...] = own[:size].astype(bf16)
    even_order, odd_order = orders(len(outs))
    for d in range(1, len(outs)):
        a, b = even_order.index(d) * size, odd_order.index(d) * size
        outs[d][...] = jnp.where(odd, other[b : b + size], other[a : a + size]).astype(bf16)


def sum_kernel(peers, blocks, capacity, relative, *refs):
    got = refs[:peers]
    base_ref, bias_ref, home_ref, out, place_ref = refs[peers:]
    place = placement(home_ref[...], blocks, capacity, relative)
    place_ref[...] = place.astype(f32).astype(bf16)
    total = base_ref[lax.axis_index("tensor")] + bias_ref[...]
    rows = total.shape[0]
    for c in range(total.shape[1] // lanes):
        part = total[:, c * lanes : (c + 1) * lanes]
        for ref in got:
            part = part + ref[c * rows : (c + 1) * rows, :].astype(f32)
        out[:, c * lanes : (c + 1) * lanes] = part


def last_kernel(pieces, *refs):
    got = refs[:pieces]
    place_ref, base_ref, cached_ref, fresh_ref, context_ref, values_ref = refs[pieces:]
    at = [0] + [1 + return_order(pieces).index(d) for d in range(1, pieces)]
    terms = jnp.concatenate([got[i][...] for i in at], axis=0)
    picked = jnp.dot(place_ref[...], terms, preferred_element_type=f32)
    values = (base_ref[...] + picked).astype(bf16)
    heads, size = values_ref.shape[1:]
    group = cached_ref.shape[1] // heads
    for h in range(heads):
        value = values[:, h * size : (h + 1) * size].astype(f32)
        values_ref[:, h, :] = value.astype(bf16)
        own = slice(h * group, (h + 1) * group)
        context = cached_ref[:, own, :] + fresh_ref[:, own, :] * value[:, None, :]
        context_ref[:, own, :] = context.astype(bf16)


def turn_kernel(in_ref, out):
    out[...] = in_ref[...].T


def base_kernel(rows_ref, matrix_ref, out):
    parts, _, width = out.shape
    for t in range(parts):
        block = matrix_ref[:, t * width : (t + 1) * width]
        out[t] = jnp.dot(rows_ref[...], block, preferred_element_type=f32)


def base_product(rows, matrix, parts):
    count, depth = rows.shape
    width = matrix.shape[1] // parts
    return call(
        base_kernel,
        "base",
        [struct((parts, count, width), f32)],
        [rows, matrix],
        2 * count * depth * matrix.shape[1],
        in_specs=[VMEM] * 2,
        out_specs=[VMEM],
    )[0]


def attention_kernel(
    length_ref, query_ref, key_ref, value_ref, new_ref, cached_ref, fresh_ref, score_ref, prob_ref
):
    requests, heads, length, size = key_ref.shape
    group = query_ref.shape[1] // heads
    scale = 1.0 / size**0.5
    count = requests * heads
    across = (((1,), (1,)), ((), ()))
    pairs = [(r, h) for r in range(requests) for h in range(heads)]
    for i, (r, h) in enumerate(pairs):
        query = query_ref[r, h * group : (h + 1) * group, :]
        score_ref[i] = lax.dot_general(query, key_ref[r, h], across, preferred_element_type=f32)
    filled = jnp.concatenate(
        [jnp.full((heads, 1, length), length_ref[r], jnp.int32) for r in range(requests)], axis=0
    )
    valid = lax.broadcasted_iota(jnp.int32, (count, group, length), 2) < filled
    scores = jnp.where(valid, score_ref[...] * scale, -1e30)
    query = query_ref[...].reshape(count, group, size).astype(f32)
    new = new_ref[...].astype(f32).reshape(count, 1, size)
    fresh = jnp.sum(query * new, axis=2, keepdims=True) * scale
    top = jnp.maximum(jnp.max(scores, axis=2, keepdims=True), fresh)
    weights = jnp.exp(scores - top)
    alone = jnp.exp(fresh - top)
    total = jnp.sum(weights, axis=2, keepdims=True) + alone
    prob_ref[...] = (weights / total).astype(bf16)
    share = jnp.broadcast_to((alone / total).astype(bf16).astype(f32), (count, group, size))
    fresh_ref[...] = share.reshape(requests, heads * group, size)
    for i, (r, h) in enumerate(pairs):
        own = slice(h * group, (h + 1) * group)
        cached_ref[r, own, :] = jnp.dot(prob_ref[i], value_ref[r, h], preferred_element_type=f32)


def attention(lengths, queries, keys, values, new_keys):
    rows, heads, length, size = keys.shape
    query_heads = queries.shape[1]
    group = query_heads // heads
    shape = struct((rows, query_heads, size), f32)
    return call(
        attention_kernel,
        "attention",
        [shape, shape],
        [lengths, queries, keys, values, new_keys],
        4 * rows * query_heads * length * size,
        in_specs=[pl.BlockSpec(memory_space=pltpu.SMEM)] + [VMEM] * 4,
        out_specs=[VMEM] * 2,
        scratch_shapes=[
            pltpu.VMEM((rows * heads, group, length), f32),
            pltpu.VMEM((rows * heads, group, length), bf16),
        ],
    )


def send(block, target):
    replicas, parts = lax.axis_size("replica"), lax.axis_size("tensor")
    pairs = []
    for r in range(replicas):
        for t in range(parts):
            to_r, to_t = target(r, t)
            pairs.append((r * parts + t, to_r * parts + to_t))
    return lax.ppermute(block, ("replica", "tensor"), pairs)


def per_device(
    activations,
    value_matrix,
    value_offset_bias,
    adapter_down_factors,
    adapter_up_factors,
    adapter_replica,
    adapter_position,
    queries,
    cached_key_rows,
    cached_value_rows,
    incoming_keys,
    lengths,
):
    rows, features = activations.shape
    replicas = lax.axis_size("replica")
    parts = lax.axis_size("tensor")
    capacity = max(2, 2 * rows // replicas)
    adapters, rank, _ = adapter_down_factors.shape
    width = value_matrix.shape[1] // parts
    heads, size = incoming_keys.shape[1:]
    slots = replicas * capacity
    direct = capacity % 16 == 0
    home_row = adapter_replica.reshape(1, rows)

    def shuffle(block):
        block = block.reshape(replicas, capacity, -1)
        block = lax.all_to_all(block, "replica", split_axis=0, concat_axis=0, tiled=True)
        return block.reshape(slots, -1)

    pieces = replicas if direct else 1
    piece = slots // pieces
    message = (piece, features + lanes)
    if direct:
        message = (piece * (features // lanes) + piece // 2, lanes)
    local_rows, *packed = call(
        functools.partial(pack_kernel, replicas, capacity, direct),
        "pack",
        [struct(activations.shape, bf16)] + [struct(message, bf16)] * pieces,
        [stay(home_row), stay(adapter_position.reshape(1, rows)), stay(activations)],
        pack_cost,
        in_specs=[HBM] * 3,
        out_specs=[VMEM] * (pieces + 1),
        scratch_shapes=[
            pltpu.VMEM((1, rows), jnp.int32),
            pltpu.VMEM((1, rows), jnp.int32),
            pltpu.SemaphoreType.DMA((3,)),
        ],
    )
    if direct:
        got = packed[:1]
        for block, a, b in list(zip(packed, *orders(replicas)))[1:]:
            got.append(send(block, lambda r, t: (r ^ (b if t % 2 else a), t)))
    else:
        got = [shuffle(packed[0])]
    base = base_product(local_rows, value_matrix, parts)
    (down,) = call(
        turn_kernel,
        "turn",
        [struct((features, adapters * rank), bf16)],
        [adapter_down_factors.reshape(adapters * rank, features)],
        200_000_000,
        in_specs=[VMEM],
        out_specs=[VMEM],
    )
    long = rows * (width // lanes) + slots // 2
    rank_own, slot_ids, *messages = call(
        functools.partial(rank_kernel, pieces, adapters),
        "rank",
        [struct((slots, rank), f32), struct((slots, rank), f32)]
        + [struct((long, lanes), bf16)] * (parts - 1),
        [*got, down, base],
        2 * slots * adapters * rank * features,
        in_specs=[VMEM] * (pieces + 2),
        out_specs=[VMEM] * (parts + 1),
    )
    heard = [send(messages[d - 1], lambda r, t: (r, t ^ d)) for d in tensor_order(parts)]
    rank_own, held_lengths = lax.optimization_barrier((rank_own, lengths))
    cached, fresh = attention(
        held_lengths, queries, cached_key_rows, cached_value_rows, incoming_keys
    )
    rank_own, cached, fresh = lax.optimization_barrier((rank_own, cached, fresh))
    up_rows = adapter_up_factors.reshape(adapters * rank, parts * width)
    terms = call(
        functools.partial(up_kernel, parts - 1, adapters, direct),
        "up",
        [struct((piece, width), bf16)] * pieces,
        [*heard, rank_own, slot_ids, up_rows],
        8 * slots * adapters * rank * width,
        in_specs=[VMEM] * (parts + 2),
        out_specs=[VMEM] * pieces,
    )
    if direct:
        returned = [terms[0]]
        for d in return_order(replicas):
            returned.append(send(terms[d], lambda r, t: (r ^ d, t ^ 1)))
    else:
        returned = [shuffle(terms[0])]
    total, place = call(
        functools.partial(sum_kernel, parts - 1, replicas, capacity, direct),
        "base_sum",
        [struct((rows, width), f32), struct((rows, slots), bf16)],
        [*heard, base, value_offset_bias.reshape(1, width), home_row],
        parts * rows * width,
        in_specs=[VMEM] * (parts + 2),
        out_specs=[VMEM] * 2,
    )
    context, values = call(
        functools.partial(last_kernel, pieces),
        "last",
        [struct(queries.shape, bf16), struct((rows, heads, size), bf16)],
        [*returned, place, total, cached, fresh],
        2 * rows * slots * width,
        in_specs=[VMEM] * (pieces + 4),
        out_specs=[VMEM] * 2,
    )
    return (context, values)


def solution(mesh):
    rows = P(("groups", "replica"))
    split = P(("groups", "replica"), "tensor")
    in_specs = (
        split,
        P("tensor", None),
        P("tensor"),
        P(("groups", "replica"), None, "tensor"),
        rows,
        rows,
        rows,
        split,
        split,
        split,
        split,
        rows,
    )
    return jax.shard_map(
        per_device, mesh=mesh, in_specs=in_specs, out_specs=(split, split), check_vma=False
    )
```

```python
import functools

import jax
import jax.numpy as jnp
from jax import lax
from jax.experimental import pallas as pl
from jax.experimental.pallas import tpu as pltpu
from jax.sharding import PartitionSpec as P

adapter_scale = 0.5
lanes = 128
f32 = jnp.float32
bf16 = jnp.bfloat16
VMEM = pl.BlockSpec(memory_space=pltpu.VMEM)
HBM = pl.BlockSpec(memory_space=pltpu.HBM)


def call(kernel, name, outs, args, flops, limit=16 << 20, **more):
    read = sum(a.size * a.dtype.itemsize for a in args)
    write = sum(o.size * o.dtype.itemsize for o in outs)
    return pl.pallas_call(
        kernel,
        name=name,
        out_shape=outs,
        cost_estimate=pl.CostEstimate(flops=flops, bytes_accessed=read + write, transcendentals=0),
        compiler_params=pltpu.CompilerParams(vmem_limit_bytes=limit),
        **more,
    )(*args)


def stay(array):
    return pltpu.with_memory_space_constraint(array, pltpu.HBM)


def struct(shape, dtype):
    return jax.ShapeDtypeStruct(shape, dtype)


def column(row):
    count = row.shape[1]
    square = lax.broadcasted_iota(jnp.int32, (count, count), 0) == lax.broadcasted_iota(
        jnp.int32, (count, count), 1
    )
    return jnp.sum(jnp.where(square, row, 0), axis=1, keepdims=True)


def orders(blocks):
    if blocks == 4:
        return [0, 2, 1, 3], [0, 2, 1, 3]
    return list(range(blocks)), list(range(blocks))


def tensor_order(parts):
    return [3, 2, 1] if parts == 4 else list(range(1, parts))


def return_order(pieces):
    return [3, 2, 1] if pieces == 4 else list(range(1, pieces))


def labels(home, blocks, relative, ordered):
    if not relative:
        return home
    step = home ^ lax.axis_index("replica")
    if not ordered:
        return step
    odd = lax.axis_index("tensor") % 2 == 1
    for at, (a, b) in enumerate(zip(*orders(blocks))):
        home = jnp.where(step == jnp.where(odd, b, a), at, home)
    return home


def placement(home_row, blocks, capacity, relative):
    home = labels(column(home_row), blocks, relative, False)
    rows = home.shape[0]
    hot = (home == lax.broadcasted_iota(jnp.int32, (rows, blocks), 1)).astype(f32)
    at = lax.broadcasted_iota(jnp.int32, (rows, rows), 0)
    below = (lax.broadcasted_iota(jnp.int32, (rows, rows), 1) < at).astype(bf16)
    before = jnp.dot(below, hot.astype(bf16), preferred_element_type=f32)
    position = jnp.sum(before * hot, axis=1, keepdims=True).astype(jnp.int32)
    flat = home * capacity + position
    return flat == lax.broadcasted_iota(jnp.int32, (rows, blocks * capacity), 1)


def pack_kernel(blocks, capacity, relative, home_hbm, slot_hbm, rows_hbm, rows_ref, *refs):
    outs, (home_ref, slot_ref, semaphores) = refs[:-3], refs[-3:]
    copies = [
        pltpu.make_async_copy(source, target, semaphores.at[i])
        for i, (source, target) in enumerate(
            [(home_hbm, home_ref), (slot_hbm, slot_ref), (rows_hbm, rows_ref)]
        )
    ]
    for copy in copies:
        copy.start()
    rows, width = rows_ref.shape
    at = lax.broadcasted_iota(jnp.int32, (rows, rows), 0)
    above = (at < lax.broadcasted_iota(jnp.int32, (rows, rows), 1)).astype(f32).astype(bf16)
    copies[0].wait()
    label = labels(home_ref[...], blocks, relative, True)
    hot = (label == lax.broadcasted_iota(jnp.int32, (blocks, rows), 0)).astype(f32)
    before = jnp.dot(hot.astype(bf16), above, preferred_element_type=f32)
    position = jnp.sum(before * hot, axis=0, keepdims=True).astype(jnp.int32)
    flat = label * capacity + position
    turned = flat == lax.broadcasted_iota(jnp.int32, (blocks * capacity, rows), 0)
    copies[1].wait()
    slots = jnp.sum(jnp.where(turned, slot_ref[...] + 1, 0).astype(f32), axis=1, keepdims=True)
    slots = jnp.broadcast_to(slots, (blocks * capacity, lanes)).astype(bf16)
    turned = turned.astype(f32).astype(bf16)
    copies[2].wait()
    packed = jnp.dot(turned, rows_ref[...], preferred_element_type=f32).astype(bf16)
    size = blocks * capacity // len(outs)
    for b, out in enumerate(outs):
        block, marks = packed[b * size : (b + 1) * size], slots[b * size : (b + 1) * size]
        if not relative:
            out[:, :width] = block
            out[:, width:] = marks
            continue
        for c in range(width // lanes):
            out[c * size : (c + 1) * size, :] = block[:, c * lanes : (c + 1) * lanes]
        half, wide = size // 2, lanes // 2
        out[size * (width // lanes) :, :] = jnp.concatenate(
            [marks[:half, :wide], marks[half:, :wide]], axis=1
        )


def rank_kernel(pieces, adapters, *refs):
    got = refs[:pieces]
    down_ref, base_ref, rank_ref, slot_ref = refs[pieces : pieces + 4]
    messages = refs[pieces + 4 :]
    features = down_ref.shape[0]
    if pieces == 1:
        rows, slots = got[0][:, :features], got[0][:, features:].astype(f32)
    else:
        size, tiles, wide = slot_ref.shape[0] // pieces, features // lanes, lanes // 2
        rows = jnp.concatenate(
            [
                jnp.concatenate([ref[c * size : (c + 1) * size, :] for ref in got], axis=0)
                for c in range(tiles)
            ],
            axis=1,
        )
        marks = [ref[tiles * size :, :].astype(f32) for ref in got]
        slots = jnp.concatenate([m[:, h : h + wide] for m in marks for h in (0, wide)], axis=0)
    slot_ref[...] = slots[:, : slot_ref.shape[1]]
    projected = jnp.dot(rows, down_ref[...], preferred_element_type=f32)
    width = down_ref.shape[1] // adapters
    total = None
    for a in range(adapters):
        term = projected[:, a * width : (a + 1) * width]
        term = jnp.where(slots[:, :width] == a + 1.0, term, 0.0)
        total = term if total is None else total + term
    rank_ref[...] = total
    half = total.shape[0] // 2
    pair = jnp.concatenate([total[:half], total[half:]], axis=1).astype(bf16)
    me = lax.axis_index("tensor")
    for d, message in enumerate(messages):
        block = base_ref[me ^ (d + 1)].astype(bf16)
        at = 0
        for c in range(block.shape[1] // lanes):
            message[at : at + block.shape[0], :] = block[:, c * lanes : (c + 1) * lanes]
            at += block.shape[0]
        message[at:, :] = pair


def up_kernel(peers, adapters, crossing, *refs):
    got = refs[:peers]
    rank_ref, slot_ref, up_ref = refs[peers : peers + 3]
    outs = refs[peers + 3 :]
    total = rank_ref[...]
    count, width = total.shape
    for ref in got:
        pair = ref[ref.shape[0] - count // 2 :, :].astype(f32)
        total = total + jnp.concatenate([pair[:, :width], pair[:, width:]], axis=0)
    slots = slot_ref[:, :width]
    wide = jnp.concatenate(
        [jnp.where(slots == a + 1.0, total, 0.0) for a in range(adapters)], axis=1
    )
    upper = wide.astype(bf16)
    lower = (wide - upper.astype(f32)).astype(bf16)
    half = outs[0].shape[1]
    first = pl.multiple_of(lax.axis_index("tensor") // 2 * 2 * half, 2 * half)
    factor = up_ref[:, pl.ds(first, 2 * half)]
    both = jnp.concatenate([upper, lower], axis=0)
    both = jnp.dot(both, factor, preferred_element_type=f32)
    term = adapter_scale * (both[:count] + both[count:])
    term = term.astype(bf16).astype(f32)
    odd = lax.axis_index("tensor") % 2 == 1
    own = jnp.where(odd, term[:, half:], term[:, :half])
    if not crossing:
        outs[0][...] = own.astype(bf16)
        return
    other = jnp.where(odd, term[:, :half], term[:, half:])
    size = outs[0].shape[0]
    outs[0][...] = own[:size].astype(bf16)
    even_order, odd_order = orders(len(outs))
    for d in range(1, len(outs)):
        a, b = even_order.index(d) * size, odd_order.index(d) * size
        outs[d][...] = jnp.where(odd, other[b : b + size], other[a : a + size]).astype(bf16)


def sum_kernel(peers, blocks, capacity, relative, *refs):
    got = refs[:peers]
    base_ref, bias_ref, home_ref, out, place_ref = refs[peers:]
    place = placement(home_ref[...], blocks, capacity, relative)
    place_ref[...] = place.astype(f32).astype(bf16)
    total = base_ref[lax.axis_index("tensor")] + bias_ref[...]
    rows = total.shape[0]
    for c in range(total.shape[1] // lanes):
        part = total[:, c * lanes : (c + 1) * lanes]
        for ref in got:
            part = part + ref[c * rows : (c + 1) * rows, :].astype(f32)
        out[:, c * lanes : (c + 1) * lanes] = part


def last_kernel(pieces, *refs):
    got = refs[:pieces]
    place_ref, base_ref, cached_ref, fresh_ref, context_ref, values_ref = refs[pieces:]
    at = [0] + [1 + return_order(pieces).index(d) for d in range(1, pieces)]
    terms = jnp.concatenate([got[i][...] for i in at], axis=0)
    picked = jnp.dot(place_ref[...], terms, preferred_element_type=f32)
    values = (base_ref[...] + picked).astype(bf16)
    heads, size = values_ref.shape[1:]
    group = cached_ref.shape[1] // heads
    for h in range(heads):
        value = values[:, h * size : (h + 1) * size].astype(f32)
        values_ref[:, h, :] = value.astype(bf16)
        own = slice(h * group, (h + 1) * group)
        context = cached_ref[:, own, :] + fresh_ref[:, own, :] * value[:, None, :]
        context_ref[:, own, :] = context.astype(bf16)


def turn_kernel(in_ref, out):
    out[...] = in_ref[...].T


def base_kernel(rows_ref, matrix_ref, out):
    parts, _, width = out.shape
    for t in range(parts):
        block = matrix_ref[:, t * width : (t + 1) * width]
        out[t] = jnp.dot(rows_ref[...], block, preferred_element_type=f32)


def base_product(rows, matrix, parts):
    count, depth = rows.shape
    width = matrix.shape[1] // parts
    return call(
        base_kernel,
        "base",
        [struct((parts, count, width), f32)],
        [rows, matrix],
        2 * count * depth * matrix.shape[1],
        in_specs=[VMEM] * 2,
        out_specs=[VMEM],
    )[0]


def attention_kernel(
    length_ref, query_ref, key_ref, value_ref, new_ref, cached_ref, fresh_ref, score_ref, prob_ref
):
    requests, heads, length, size = key_ref.shape
    group = query_ref.shape[1] // heads
    scale = 1.0 / size**0.5
    count = requests * heads
    across = (((1,), (1,)), ((), ()))
    pairs = [(r, h) for r in range(requests) for h in range(heads)]
    for i, (r, h) in enumerate(pairs):
        query = query_ref[r, h * group : (h + 1) * group, :]
        score_ref[i] = lax.dot_general(query, key_ref[r, h], across, preferred_element_type=f32)
    filled = jnp.concatenate(
        [jnp.full((heads, 1, length), length_ref[r], jnp.int32) for r in range(requests)], axis=0
    )
    valid = lax.broadcasted_iota(jnp.int32, (count, group, length), 2) < filled
    scores = jnp.where(valid, score_ref[...] * scale, -1e30)
    query = query_ref[...].reshape(count, group, size).astype(f32)
    new = new_ref[...].astype(f32).reshape(count, 1, size)
    fresh = jnp.sum(query * new, axis=2, keepdims=True) * scale
    top = jnp.maximum(jnp.max(scores, axis=2, keepdims=True), fresh)
    weights = jnp.exp(scores - top)
    alone = jnp.exp(fresh - top)
    total = jnp.sum(weights, axis=2, keepdims=True) + alone
    prob_ref[...] = (weights / total).astype(bf16)
    share = jnp.broadcast_to((alone / total).astype(bf16).astype(f32), (count, group, size))
    fresh_ref[...] = share.reshape(requests, heads * group, size)
    for i, (r, h) in enumerate(pairs):
        own = slice(h * group, (h + 1) * group)
        cached_ref[r, own, :] = jnp.dot(prob_ref[i], value_ref[r, h], preferred_element_type=f32)


def attention(lengths, queries, keys, values, new_keys):
    rows, heads, length, size = keys.shape
    query_heads = queries.shape[1]
    group = query_heads // heads
    shape = struct((rows, query_heads, size), f32)
    return call(
        attention_kernel,
        "attention",
        [shape, shape],
        [lengths, queries, keys, values, new_keys],
        4 * rows * query_heads * length * size,
        in_specs=[pl.BlockSpec(memory_space=pltpu.SMEM)] + [VMEM] * 4,
        out_specs=[VMEM] * 2,
        scratch_shapes=[
            pltpu.VMEM((rows * heads, group, length), f32),
            pltpu.VMEM((rows * heads, group, length), bf16),
        ],
    )


def send(block, target):
    replicas, parts = lax.axis_size("replica"), lax.axis_size("tensor")
    pairs = []
    for r in range(replicas):
        for t in range(parts):
            to_r, to_t = target(r, t)
            pairs.append((r * parts + t, to_r * parts + to_t))
    return lax.ppermute(block, ("replica", "tensor"), pairs)


def per_device(
    activations,
    value_matrix,
    value_offset_bias,
    adapter_down_factors,
    adapter_up_factors,
    adapter_replica,
    adapter_position,
    queries,
    cached_key_rows,
    cached_value_rows,
    incoming_keys,
    lengths,
):
    rows, features = activations.shape
    replicas = lax.axis_size("replica")
    parts = lax.axis_size("tensor")
    capacity = max(2, 2 * rows // replicas)
    adapters, rank, _ = adapter_down_factors.shape
    width = value_matrix.shape[1] // parts
    heads, size = incoming_keys.shape[1:]
    slots = replicas * capacity
    direct = capacity % 16 == 0
    home_row = adapter_replica.reshape(1, rows)

    def shuffle(block):
        block = block.reshape(replicas, capacity, -1)
        block = lax.all_to_all(block, "replica", split_axis=0, concat_axis=0, tiled=True)
        return block.reshape(slots, -1)

    pieces = replicas if direct else 1
    piece = slots // pieces
    message = (piece, features + lanes)
    if direct:
        message = (piece * (features // lanes) + piece // 2, lanes)
    local_rows, *packed = call(
        functools.partial(pack_kernel, replicas, capacity, direct),
        "pack",
        [struct(activations.shape, bf16)] + [struct(message, bf16)] * pieces,
        [stay(home_row), stay(adapter_position.reshape(1, rows)), stay(activations)],
        2 * rows * slots * features,
        in_specs=[HBM] * 3,
        out_specs=[VMEM] * (pieces + 1),
        scratch_shapes=[
            pltpu.VMEM((1, rows), jnp.int32),
            pltpu.VMEM((1, rows), jnp.int32),
            pltpu.SemaphoreType.DMA((3,)),
        ],
    )
    if direct:
        got = packed[:1]
        for block, a, b in list(zip(packed, *orders(replicas)))[1:]:
            got.append(send(block, lambda r, t: (r ^ (b if t % 2 else a), t)))
    else:
        got = [shuffle(packed[0])]
    base = base_product(local_rows, value_matrix, parts)
    (down,) = call(
        turn_kernel,
        "turn",
        [struct((features, adapters * rank), bf16)],
        [adapter_down_factors.reshape(adapters * rank, features)],
        200_000_000,
        in_specs=[VMEM],
        out_specs=[VMEM],
    )
    long = rows * (width // lanes) + slots // 2
    rank_own, slot_ids, *messages = call(
        functools.partial(rank_kernel, pieces, adapters),
        "rank",
        [struct((slots, rank), f32), struct((slots, rank), f32)]
        + [struct((long, lanes), bf16)] * (parts - 1),
        [*got, down, base],
        2 * slots * adapters * rank * features,
        in_specs=[VMEM] * (pieces + 2),
        out_specs=[VMEM] * (parts + 1),
    )
    heard = [send(messages[d - 1], lambda r, t: (r, t ^ d)) for d in tensor_order(parts)]
    rank_own, held_lengths = lax.optimization_barrier((rank_own, lengths))
    cached, fresh = attention(
        held_lengths, queries, cached_key_rows, cached_value_rows, incoming_keys
    )
    rank_own, cached, fresh = lax.optimization_barrier((rank_own, cached, fresh))
    up_rows = adapter_up_factors.reshape(adapters * rank, parts * width)
    terms = call(
        functools.partial(up_kernel, parts - 1, adapters, direct),
        "up",
        [struct((piece, width), bf16)] * pieces,
        [*heard, rank_own, slot_ids, up_rows],
        8 * slots * adapters * rank * width,
        in_specs=[VMEM] * (parts + 2),
        out_specs=[VMEM] * pieces,
    )
    if direct:
        returned = [terms[0]]
        for d in return_order(replicas):
            returned.append(send(terms[d], lambda r, t: (r ^ d, t ^ 1)))
    else:
        returned = [shuffle(terms[0])]
    total, place = call(
        functools.partial(sum_kernel, parts - 1, replicas, capacity, direct),
        "base_sum",
        [struct((rows, width), f32), struct((rows, slots), bf16)],
        [*heard, base, value_offset_bias.reshape(1, width), home_row],
        parts * rows * width,
        in_specs=[VMEM] * (parts + 2),
        out_specs=[VMEM] * 2,
    )
    context, values = call(
        functools.partial(last_kernel, pieces),
        "last",
        [struct(queries.shape, bf16), struct((rows, heads, size), bf16)],
        [*returned, place, total, cached, fresh],
        2 * rows * slots * width,
        in_specs=[VMEM] * (pieces + 4),
        out_specs=[VMEM] * 2,
    )
    return (context, values)


def solution(mesh):
    rows = P(("groups", "replica"))
    split = P(("groups", "replica"), "tensor")
    in_specs = (
        split,
        P("tensor", None),
        P("tensor"),
        P(("groups", "replica"), None, "tensor"),
        rows,
        rows,
        rows,
        split,
        split,
        split,
        split,
        rows,
    )
    return jax.shard_map(
        per_device, mesh=mesh, in_specs=in_specs, out_specs=(split, split), check_vma=False
    )
```
